512 devices in a mesh: rep: 4 (over y_lo, core), fsdp: 128 (over z, y_hi, x).
Axes of the slice: x: 4, y: 4 (y_hi: 2, y_lo: 2; y = y_hi * 2 + y_lo), z: 16, core: 2. Of those that a mesh axis runs over, the one named last changes fastest.
Arguments:
- hidden_in: bfloat16 [4, 24576, 8192], P('rep', 'fsdp'), may hold values from -6 to 6
- norm_gain: float32 [8192], replicated, may hold values from 0.1 to 1.9
- key_weight: bfloat16 [4, 8192, 512], P('rep', 'fsdp'), may hold values from -0.0625 to 0.0625
- fragment_index: int32 [1], replicated, may hold values from 0 to 6
- outer_params: float32 [7, 8192, 512], P(None, 'fsdp'), may hold values from -6 to 6
- outer_moment: float32 [7, 8192, 512], P(None, 'fsdp'), may hold values from -4 to 4
- inner_params: bfloat16 [4, 7, 8192, 512], P('rep', None, 'fsdp'), may hold values from -6 to 6
Outputs:
- keys: bfloat16 [4, 24576, 512], P('rep', 'fsdp')
- new_outer: float32 [8192, 512], P('fsdp')
- new_moment: float32 [8192, 512], P('fsdp')
- mixed_inner: bfloat16 [4, 8192, 512], P('rep', 'fsdp')
The draws below stay inside these ranges and needn't reach their ends.
All inputs are finite; a program needn't handle non-finite values.
Results may differ from the reference program's by a relative error of at most 0.022.
Values may be sent and summed in bfloat16 or wider, within the bound.
No kernel may reach another device: no remote copies, remote signals or barrier semaphores. Data moves between devices by JAX's collectives and lax.ppermute only.
A program may use at most 64 MiB of HBM per device.

```python
import jax
import jax.numpy as jnp
from jax import lax

D = 8192
KVW = 512
FRAG_LAYERS = 7
TOKENS = 24576
N_REP = 4


def levels(rng, shape, pieces, smallest, high):
    loudness, own = 1.0, jax.random.fold_in(rng, 6)
    for axis_at, shards_of in pieces:
        draws = jnp.exp(jax.random.uniform(jax.random.fold_in(own, axis_at), (shards_of,), jnp.float32, smallest / len(pieces), high / len(pieces)))
        loudness = loudness * jnp.repeat(draws, shape[axis_at] // shards_of).reshape([-1 if axis == axis_at else 1 for axis in range(len(shape))])
    return loudness


def normal_values(rng, extent, deviation, reach, split=(), kind=jnp.bfloat16):
    values = jax.random.normal(rng, extent, jnp.float32) * deviation
    if len(split) > 0:
        values = levels(rng, extent, split, -0.22, 0.18) * values
    return jnp.clip(values, min=-reach, max=reach).astype(kind)


def setup_inputs(seed: int = 0) -> dict:
    arg_keys = jax.random.split(jax.random.key(seed), 8)
    hidden_in = normal_values(arg_keys[0], (N_REP, TOKENS, D), 1.0, 6.0, ((0, 4), (1, 128)))
    norm_gain = jnp.clip(1.0 + 0.18 * jax.random.normal(arg_keys[1], (D,), jnp.float32), 0.1, 1.9)
    key_weight = normal_values(arg_keys[2], (N_REP, D, KVW), D ** -0.5, 0.0625, ((0, 4), (1, 128)))
    fragment_index = jax.random.randint(arg_keys[3], (1,), 0, FRAG_LAYERS).astype(jnp.int32)
    outer_params = normal_values(arg_keys[4], (FRAG_LAYERS, D, KVW), 1.0, 6.0, ((1, 128),), jnp.float32)
    outer_moment = normal_values(arg_keys[5], (FRAG_LAYERS, D, KVW), 0.5, 4.0, ((1, 128),), jnp.float32)
    inner_params = normal_values(arg_keys[6], (N_REP, FRAG_LAYERS, D, KVW), 1.0, 6.0, ((0, 4), (2, 128)))
    return {"hidden_in": hidden_in, "norm_gain": norm_gain, "key_weight": key_weight, "fragment_index": fragment_index, "outer_params": outer_params, "outer_moment": outer_moment, "inner_params": inner_params}


momentum_coef = 0.9
outer_rate = 0.7
mix_keep = 0.5
epsilon = 1e-05

def project_keys(pair):
    hidden, weight, gain = pair
    hidden32 = hidden.astype(jnp.float32)
    mean_square = lax.optimization_barrier(jnp.mean(hidden32 * hidden32, axis=-1, keepdims=True))
    normed = (hidden32 * lax.rsqrt(mean_square + epsilon) * gain).astype(jnp.bfloat16)
    return jnp.dot(normed, weight, preferred_element_type=jnp.float32).astype(jnp.bfloat16)

def reference(hidden_in, norm_gain, key_weight, fragment_index, outer_params, outer_moment, inner_params):
    layer_idx = fragment_index[0]
    outer_layer = lax.dynamic_index_in_dim(outer_params, layer_idx, 0, keepdims=False)
    moment_layer = lax.dynamic_index_in_dim(outer_moment, layer_idx, 0, keepdims=False)
    inner_layer = lax.dynamic_index_in_dim(inner_params, layer_idx, 1, keepdims=False)
    pseudo_grad = (outer_layer[None] - inner_layer.astype(jnp.float32)).astype(jnp.bfloat16)
    averaged = lax.optimization_barrier(jnp.sum(pseudo_grad.astype(jnp.float32), axis=0)) / N_REP
    new_moment = momentum_coef * moment_layer + averaged
    new_outer = outer_layer - outer_rate * (averaged + momentum_coef * new_moment)
    mixed_inner = (mix_keep * inner_layer.astype(jnp.float32) + (1.0 - mix_keep) * new_outer[None]).astype(jnp.bfloat16)
    gains = jnp.broadcast_to(norm_gain[None], (hidden_in.shape[0], norm_gain.shape[0]))
    keys = lax.map(project_keys, (hidden_in, key_weight, gains))
    return (keys, new_outer, new_moment, mixed_inner)
```

```python
import jax
import jax.numpy as jnp
from jax import lax
from jax.experimental import pallas as pl
from jax.experimental.pallas import tpu as pltpu
from jax.sharding import Mesh, PartitionSpec as P

momentum_coef = 0.9
outer_rate = 0.7
mix_keep = 0.5
epsilon = 1e-05

Z, PLANE, REP = "z", ("yh", "x"), ("yl", "core")
PLANES, PEERS = 16, 8
ROWS = 32


def outer_update(averaged, outer_layer, moment_layer):
    new_moment = momentum_coef * moment_layer + averaged
    new_outer = outer_layer - outer_rate * (averaged + momentum_coef * new_moment)
    return (new_outer, new_moment)


def pack_kernel(hidden_ref, packed_ref, scale_ref):
    hidden = hidden_ref[...].astype(jnp.float32)
    features = hidden.shape[1]
    mean_square = jnp.sum(hidden * hidden, axis=-1, keepdims=True) / features
    scale_ref[...] = lax.rsqrt(mean_square + epsilon)
    low = lax.broadcasted_iota(jnp.int32, (hidden.shape[0], 128), 1) < 64
    for pair in range(PLANES // 2):
        for tile in range(PEERS // 2):
            start = pair * 1024 + tile * 128
            first = hidden[:, start : start + 128]
            second = hidden[:, start + 512 : start + 640]
            columns = slice(pair * 128, pair * 128 + 128)
            even = jnp.where(low, first, pltpu.roll(second, 64, 1))
            odd = jnp.where(low, pltpu.roll(first, 64, 1), second)
            packed_ref[2 * tile, :, columns] = even.astype(jnp.bfloat16)
            packed_ref[2 * tile + 1, :, columns] = odd.astype(jnp.bfloat16)


def pack(hidden):
    tokens, features = hidden.shape
    return pl.pallas_call(
        pack_kernel,
        grid=(tokens // ROWS,),
        in_specs=[pl.BlockSpec((ROWS, features), lambda i: (i, 0))],
        out_specs=[
            pl.BlockSpec((PEERS, ROWS, features // PEERS), lambda i: (0, i, 0)),
            pl.BlockSpec((ROWS, 1), lambda i: (i, 0)),
        ],
        out_shape=[
            jax.ShapeDtypeStruct((PEERS, tokens, features // PEERS), jnp.bfloat16),
            jax.ShapeDtypeStruct((tokens, 1), jnp.float32),
        ],
        compiler_params=pltpu.CompilerParams(vmem_limit_bytes=16 * 1024 * 1024),
        cost_estimate=pl.CostEstimate(
            flops=4 * tokens * features, bytes_accessed=4 * tokens * features, transcendentals=tokens
        ),
        name="pack_hidden",
    )(hidden)


def shards(
    hidden_in, norm_gain, key_weight, fragment_index, outer_params, outer_moment, inner_params
):
    replicas = 4
    layer_idx = fragment_index[0]
    outer_layer = lax.dynamic_index_in_dim(outer_params, layer_idx, 0, keepdims=False)
    moment_layer = lax.dynamic_index_in_dim(outer_moment, layer_idx, 0, keepdims=False)
    inner_layer = lax.dynamic_index_in_dim(inner_params[0], layer_idx, 0, keepdims=False)
    pseudo_grad = (outer_layer - inner_layer.astype(jnp.float32)).astype(jnp.bfloat16)
    every = lax.all_gather(pseudo_grad, REP, axis=0, tiled=False)
    summed = jnp.sum(every.astype(jnp.float32), axis=0)
    new_outer, new_moment = outer_update(summed / replicas, outer_layer, moment_layer)
    mixed_inner = (
        mix_keep * inner_layer.astype(jnp.float32) + (1.0 - mix_keep) * new_outer
    ).astype(jnp.bfloat16)

    weight = lax.all_gather(key_weight[0], Z, axis=0, tiled=True)
    packed, scale = pack(hidden_in[0])
    gathered = lax.all_to_all(packed, PLANE, 0, 0, tiled=True)
    mine = lax.axis_index(PLANE)
    gain = lax.dynamic_index_in_dim(norm_gain.reshape(PLANES, PEERS, 64), mine, 1, keepdims=False)
    weight = (weight.astype(jnp.float32) * gain.reshape(-1, 1)).astype(jnp.bfloat16)
    tokens = gathered.reshape(-1, gathered.shape[-1])
    partial = jnp.dot(tokens, weight, preferred_element_type=jnp.float32).astype(jnp.bfloat16)
    partial = partial.reshape(PEERS, -1, partial.shape[-1])
    partial = lax.all_to_all(partial, PLANE, 0, 0, tiled=True)
    keys = (jnp.sum(partial.astype(jnp.float32), axis=0) * scale).astype(jnp.bfloat16)
    return (keys[None], new_outer, new_moment, mixed_inner[None])


def solution(mesh):
    fine = Mesh(mesh.devices.reshape(2, 2, 16, 2, 4), ("yl", "core", "z", "yh", "x"))
    fsdp = ("z", "yh", "x")
    placed = (
        P(REP, fsdp, None),
        P(),
        P(REP, fsdp, None),
        P(),
        P(None, fsdp, None),
        P(None, fsdp, None),
        P(REP, None, fsdp, None),
    )
    return jax.shard_map(
        shards,
        mesh=fine,
        in_specs=placed,
        out_specs=(
            P(REP, fsdp, None),
            P(fsdp, None),
            P(fsdp, None),
            P(REP, fsdp, None),
        ),
        check_vma=False,
    )
```

```python
import jax
import jax.numpy as jnp
from jax import lax
from jax.experimental import pallas as pl
from jax.experimental.pallas import tpu as pltpu
from jax.sharding import Mesh, PartitionSpec as P

momentum_coef = 0.9
outer_rate = 0.7
mix_keep = 0.5
epsilon = 1e-05

Z, PLANE, REP = "z", ("yh", "x"), ("yl", "core")
PLANES, PEERS = 16, 8
ROWS = 32


def outer_update(averaged, outer_layer, moment_layer):
    new_moment = momentum_coef * moment_layer + averaged
    new_outer = outer_layer - outer_rate * (averaged + momentum_coef * new_moment)
    return (new_outer, new_moment)


def pack_kernel(hidden_ref, gain_ref, packed_ref, scale_ref):
    hidden = hidden_ref[...].astype(jnp.float32)
    features = hidden.shape[1]
    mean_square = jnp.sum(hidden * hidden, axis=-1, keepdims=True) / features
    scale_ref[...] = lax.rsqrt(mean_square + epsilon)
    gained = hidden * gain_ref[...]
    low = lax.broadcasted_iota(jnp.int32, (hidden.shape[0], 128), 1) < 64
    for pair in range(PLANES // 2):
        for tile in range(PEERS // 2):
            start = pair * 1024 + tile * 128
            first = gained[:, start : start + 128]
            second = gained[:, start + 512 : start + 640]
            columns = slice(pair * 128, pair * 128 + 128)
            even = jnp.where(low, first, pltpu.roll(second, 64, 1))
            odd = jnp.where(low, pltpu.roll(first, 64, 1), second)
            packed_ref[2 * tile, :, columns] = even.astype(jnp.bfloat16)
            packed_ref[2 * tile + 1, :, columns] = odd.astype(jnp.bfloat16)


def pack(hidden, gain):
    tokens, features = hidden.shape
    return pl.pallas_call(
        pack_kernel,
        grid=(tokens // ROWS,),
        in_specs=[
            pl.BlockSpec((ROWS, features), lambda i: (i, 0)),
            pl.BlockSpec((1, features), lambda i: (0, 0)),
        ],
        out_specs=[
            pl.BlockSpec((PEERS, ROWS, features // PEERS), lambda i: (0, i, 0)),
            pl.BlockSpec((ROWS, 1), lambda i: (i, 0)),
        ],
        out_shape=[
            jax.ShapeDtypeStruct((PEERS, tokens, features // PEERS), jnp.bfloat16),
            jax.ShapeDtypeStruct((tokens, 1), jnp.float32),
        ],
        compiler_params=pltpu.CompilerParams(vmem_limit_bytes=16 * 1024 * 1024),
        cost_estimate=pl.CostEstimate(
            flops=4 * tokens * features, bytes_accessed=4 * tokens * features, transcendentals=tokens
        ),
        name="pack_hidden",
    )(hidden, gain)


HELD = ((0, -4, 4, 8), (-1, -5, 3, 7), (1, -3, 5, 9), (-2, -6), (2, 6))


def project_kernel(place_ref, tokens_ref, *refs):
    held_refs, (out_ref, weight) = refs[: len(HELD)], refs[len(HELD) :]

    @pl.when(pl.program_id(0) == 0)
    def _():
        for held_ref, offsets in zip(held_refs, HELD, strict=True):
            for at, offset in enumerate(offsets):
                plane = lax.rem(place_ref[0] + offset + PLANES, PLANES)
                rows = pl.ds(pl.multiple_of(plane * 64, 64), 64)
                weight[rows, :] = held_ref[at * 64 : at * 64 + 64, :]

    out_ref[0] = jnp.dot(tokens_ref[0], weight[...], preferred_element_type=jnp.float32).astype(
        jnp.bfloat16
    )


def project(place, tokens, held):
    peers, rows, features = tokens.shape
    width = held[0].shape[1]
    whole = [pl.BlockSpec(part.shape, lambda i, place: (0, 0)) for part in held]
    return pl.pallas_call(
        project_kernel,
        grid_spec=pltpu.PrefetchScalarGridSpec(
            num_scalar_prefetch=1,
            grid=(peers,),
            in_specs=[pl.BlockSpec((1, rows, features), lambda i, place: (i, 0, 0)), *whole],
            out_specs=pl.BlockSpec((1, rows, width), lambda i, place: (i, 0, 0)),
            scratch_shapes=[pltpu.VMEM((features, width), jnp.bfloat16)],
        ),
        out_shape=jax.ShapeDtypeStruct((peers, rows, width), jnp.bfloat16),
        compiler_params=pltpu.CompilerParams(vmem_limit_bytes=16 * 1024 * 1024),
        cost_estimate=pl.CostEstimate(
            flops=2 * peers * rows * features * width,
            bytes_accessed=2 * (peers * rows * (features + width) + features * width),
            transcendentals=0,
        ),
        name="project_keys",
    )(place, tokens, *held)


def moved(block, steps):
    return lax.ppermute(block, Z, [(z, (z + steps) % PLANES) for z in range(PLANES)])


def weight_blocks(block):
    below, above, across = moved(block, 4), moved(block, -4), moved(block, 8)
    own = jnp.concatenate([block, below, above, across], axis=0)
    return (
        own,
        moved(own, 1),
        moved(own, -1),
        moved(jnp.concatenate([block, below], axis=0), 2),
        moved(jnp.concatenate([block, above], axis=0), -2),
    )


def shards(
    hidden_in, norm_gain, key_weight, fragment_index, outer_params, outer_moment, inner_params
):
    replicas = 4
    layer_idx = fragment_index[0]
    outer_layer = lax.dynamic_index_in_dim(outer_params, layer_idx, 0, keepdims=False)
    moment_layer = lax.dynamic_index_in_dim(outer_moment, layer_idx, 0, keepdims=False)
    inner_layer = lax.dynamic_index_in_dim(inner_params[0], layer_idx, 0, keepdims=False)
    pseudo_grad = (outer_layer - inner_layer.astype(jnp.float32)).astype(jnp.bfloat16)
    every = lax.all_gather(pseudo_grad, REP, axis=0, tiled=False)
    summed = jnp.sum(every.astype(jnp.float32), axis=0)
    new_outer, new_moment = outer_update(summed / replicas, outer_layer, moment_layer)
    mixed_inner = (
        mix_keep * inner_layer.astype(jnp.float32) + (1.0 - mix_keep) * new_outer
    ).astype(jnp.bfloat16)

    held = weight_blocks(key_weight[0])
    packed, scale = pack(hidden_in[0], norm_gain[None])
    tokens = lax.all_to_all(packed, PLANE, 0, 0, tiled=True)
    tokens, new_outer, new_moment, mixed_inner = lax.optimization_barrier(
        (tokens, new_outer, new_moment, mixed_inner)
    )
    place = lax.axis_index(Z).astype(jnp.int32)[None]
    partial = lax.all_to_all(project(place, tokens, held), PLANE, 0, 0, tiled=True)
    keys = (jnp.sum(partial.astype(jnp.float32), axis=0) * scale).astype(jnp.bfloat16)
    return (keys[None], new_outer, new_moment, mixed_inner[None])


def solution(mesh):
    fine = Mesh(mesh.devices.reshape(2, 2, 16, 2, 4), ("yl", "core", "z", "yh", "x"))
    fsdp = ("z", "yh", "x")
    placed = (
        P(REP, fsdp, None),
        P(),
        P(REP, fsdp, None),
        P(),
        P(None, fsdp, None),
        P(None, fsdp, None),
        P(REP, None, fsdp, None),
    )
    return jax.shard_map(
        shards,
        mesh=fine,
        in_specs=placed,
        out_specs=(
            P(REP, fsdp, None),
            P(fsdp, None),
            P(fsdp, None),
            P(REP, fsdp, None),
        ),
        check_vma=False,
    )
```

```python
import jax
import jax.numpy as jnp
from jax import lax
from jax.experimental import pallas as pl
from jax.experimental.pallas import tpu as pltpu
from jax.sharding import Mesh, PartitionSpec as P

momentum_coef = 0.9
outer_rate = 0.7
mix_keep = 0.5
epsilon = 1e-05

Z, PLANE, REP = "z", ("yh", "x"), ("yl", "core")
PLANES, PEERS = 16, 8
ROWS, SOURCES = 32, 2


def outer_update(averaged, outer_layer, moment_layer):
    new_moment = momentum_coef * moment_layer + averaged
    new_outer = outer_layer - outer_rate * (averaged + momentum_coef * new_moment)
    return (new_outer, new_moment)


def pack_kernel(hidden_ref, gain_ref, packed_ref, scale_ref):
    hidden = hidden_ref[...].astype(jnp.float32)
    features = hidden.shape[1]
    mean_square = jnp.sum(hidden * hidden, axis=-1, keepdims=True) / features
    scale_ref[...] = lax.rsqrt(mean_square + epsilon)
    gained = hidden * gain_ref[...]
    low = lax.broadcasted_iota(jnp.int32, (hidden.shape[0], 128), 1) < 64
    for pair in range(PLANES // 2):
        for tile in range(PEERS // 2):
            start = pair * 1024 + tile * 128
            first = gained[:, start : start + 128]
            second = gained[:, start + 512 : start + 640]
            columns = slice(pair * 128, pair * 128 + 128)
            even = jnp.where(low, first, pltpu.roll(second, 64, 1))
            odd = jnp.where(low, pltpu.roll(first, 64, 1), second)
            packed_ref[2 * tile, :, columns] = even.astype(jnp.bfloat16)
            packed_ref[2 * tile + 1, :, columns] = odd.astype(jnp.bfloat16)


def pack(hidden, gain):
    tokens, features = hidden.shape
    return pl.pallas_call(
        pack_kernel,
        grid=(tokens // ROWS,),
        in_specs=[
            pl.BlockSpec((ROWS, features), lambda i: (i, 0)),
            pl.BlockSpec((1, features), lambda i: (0, 0)),
        ],
        out_specs=[
            pl.BlockSpec((PEERS, ROWS, features // PEERS), lambda i: (0, i, 0)),
            pl.BlockSpec((ROWS, 1), lambda i: (i, 0)),
        ],
        out_shape=[
            jax.ShapeDtypeStruct((PEERS, tokens, features // PEERS), jnp.bfloat16),
            jax.ShapeDtypeStruct((tokens, 1), jnp.float32),
        ],
        compiler_params=pltpu.CompilerParams(vmem_limit_bytes=16 * 1024 * 1024),
        cost_estimate=pl.CostEstimate(
            flops=4 * tokens * features, bytes_accessed=4 * tokens * features, transcendentals=tokens
        ),
        name="pack_hidden",
    )(hidden, gain)


HELD = ((0, -4, 4, 8), (-1, -5, 3, 7), (1, -3, 5, 9), (-2, -6), (2, 6))


def project_kernel(place_ref, tokens_ref, *refs):
    held_refs, (out_ref, weight) = refs[: len(HELD)], refs[len(HELD) :]

    @pl.when(pl.program_id(0) == 0)
    def _():
        for held_ref, offsets in zip(held_refs, HELD, strict=True):
            for at, offset in enumerate(offsets):
                plane = lax.rem(place_ref[0] + offset + PLANES, PLANES)
                rows = pl.ds(pl.multiple_of(plane * 64, 64), 64)
                weight[rows, :] = held_ref[at * 64 : at * 64 + 64, :]

    tokens = tokens_ref[...].reshape(-1, tokens_ref.shape[-1])
    product = jnp.dot(tokens, weight[...], preferred_element_type=jnp.float32)
    out_ref[...] = product.astype(jnp.bfloat16).reshape(out_ref.shape)


def project(place, tokens, held):
    peers, rows, features = tokens.shape
    width = held[0].shape[1]
    whole = [pl.BlockSpec(part.shape, lambda i, place: (0, 0)) for part in held]
    return pl.pallas_call(
        project_kernel,
        grid_spec=pltpu.PrefetchScalarGridSpec(
            num_scalar_prefetch=1,
            grid=(peers // SOURCES,),
            in_specs=[pl.BlockSpec((SOURCES, rows, features), lambda i, place: (i, 0, 0)), *whole],
            out_specs=pl.BlockSpec((SOURCES, rows, width), lambda i, place: (i, 0, 0)),
            scratch_shapes=[pltpu.VMEM((features, width), jnp.bfloat16)],
        ),
        out_shape=jax.ShapeDtypeStruct((peers, rows, width), jnp.bfloat16),
        compiler_params=pltpu.CompilerParams(vmem_limit_bytes=16 * 1024 * 1024),
        cost_estimate=pl.CostEstimate(
            flops=2 * peers * rows * features * width,
            bytes_accessed=2 * (peers * rows * (features + width) + features * width),
            transcendentals=0,
        ),
        name="project_keys",
    )(place, tokens, *held)


def moved(block, steps):
    return lax.ppermute(block, Z, [(z, (z + steps) % PLANES) for z in range(PLANES)])


def weight_blocks(block):
    below, above, across = moved(block, 4), moved(block, -4), moved(block, 8)
    own = jnp.concatenate([block, below, above, across], axis=0)
    return (
        own,
        moved(own, 1),
        moved(own, -1),
        moved(jnp.concatenate([block, below], axis=0), 2),
        moved(jnp.concatenate([block, above], axis=0), -2),
    )


def shards(
    hidden_in, norm_gain, key_weight, fragment_index, outer_params, outer_moment, inner_params
):
    replicas = 4
    layer_idx = fragment_index[0]
    outer_layer = lax.dynamic_index_in_dim(outer_params, layer_idx, 0, keepdims=False)
    moment_layer = lax.dynamic_index_in_dim(outer_moment, layer_idx, 0, keepdims=False)
    inner_layer = lax.dynamic_index_in_dim(inner_params[0], layer_idx, 0, keepdims=False)
    pseudo_grad = (outer_layer - inner_layer.astype(jnp.float32)).astype(jnp.bfloat16)
    held = weight_blocks(key_weight[0])
    packed, scale = pack(hidden_in[0], norm_gain[None])
    tokens = lax.all_to_all(packed, PLANE, 0, 0, tiled=True)
    place = lax.axis_index(Z).astype(jnp.int32)[None]
    partial = project(place, tokens, held)
    partial, pseudo_grad = lax.optimization_barrier((partial, pseudo_grad))
    partial = lax.all_to_all(partial, PLANE, 0, 0, tiled=True)
    every = lax.all_gather(pseudo_grad, REP, axis=0, tiled=False)
    summed = jnp.sum(every.astype(jnp.float32), axis=0)
    new_outer, new_moment = outer_update(summed / replicas, outer_layer, moment_layer)
    mixed_inner = (
        mix_keep * inner_layer.astype(jnp.float32) + (1.0 - mix_keep) * new_outer
    ).astype(jnp.bfloat16)
    keys = (jnp.sum(partial.astype(jnp.float32), axis=0) * scale).astype(jnp.bfloat16)
    return (keys[None], new_outer, new_moment, mixed_inner[None])


def solution(mesh):
    fine = Mesh(mesh.devices.reshape(2, 2, 16, 2, 4), ("yl", "core", "z", "yh", "x"))
    fsdp = ("z", "yh", "x")
    placed = (
        P(REP, fsdp, None),
        P(),
        P(REP, fsdp, None),
        P(),
        P(None, fsdp, None),
        P(None, fsdp, None),
        P(REP, None, fsdp, None),
    )
    return jax.shard_map(
        shards,
        mesh=fine,
        in_specs=placed,
        out_specs=(
            P(REP, fsdp, None),
            P(fsdp, None),
            P(fsdp, None),
            P(REP, fsdp, None),
        ),
        check_vma=False,
    )
```

```python
import jax
import jax.numpy as jnp
from jax import lax
from jax.experimental import pallas as pl
from jax.experimental.pallas import tpu as pltpu
from jax.sharding import Mesh, PartitionSpec as P

momentum_coef = 0.9
outer_rate = 0.7
mix_keep = 0.5
epsilon = 1e-05

Z, PLANE, REP = "z", ("yh", "x"), ("yl", "core")
PLANES, PEERS = 16, 8
ROWS, SOURCES = 32, 2
PACK_VMEM, PROJECT_VMEM = 60 * 1024 * 1024, 60 * 1024 * 1024


def outer_update(averaged, outer_layer, moment_layer):
    new_moment = momentum_coef * moment_layer + averaged
    new_outer = outer_layer - outer_rate * (averaged + momentum_coef * new_moment)
    return (new_outer, new_moment)


def pack_kernel(hidden_ref, gain_ref, packed_ref, scale_ref):
    hidden = hidden_ref[...].astype(jnp.float32)
    features = hidden.shape[1]
    mean_square = jnp.sum(hidden * hidden, axis=-1, keepdims=True) / features
    scale_ref[...] = lax.rsqrt(mean_square + epsilon)
    gained = hidden * gain_ref[...]
    low = lax.broadcasted_iota(jnp.int32, (hidden.shape[0], 128), 1) < 64
    for pair in range(PLANES // 2):
        for tile in range(PEERS // 2):
            start = pair * 1024 + tile * 128
            first = gained[:, start : start + 128]
            second = gained[:, start + 512 : start + 640]
            columns = slice(pair * 128, pair * 128 + 128)
            even = jnp.where(low, first, pltpu.roll(second, 64, 1))
            odd = jnp.where(low, pltpu.roll(first, 64, 1), second)
            packed_ref[2 * tile, :, columns] = even.astype(jnp.bfloat16)
            packed_ref[2 * tile + 1, :, columns] = odd.astype(jnp.bfloat16)


def pack(hidden, gain):
    tokens, features = hidden.shape
    return pl.pallas_call(
        pack_kernel,
        grid=(tokens // ROWS,),
        in_specs=[
            pl.BlockSpec((ROWS, features), lambda i: (i, 0)),
            pl.BlockSpec((1, features), lambda i: (0, 0)),
        ],
        out_specs=[
            pl.BlockSpec((PEERS, ROWS, features // PEERS), lambda i: (0, i, 0)),
            pl.BlockSpec((ROWS, 1), lambda i: (i, 0)),
        ],
        out_shape=[
            jax.ShapeDtypeStruct((PEERS, tokens, features // PEERS), jnp.bfloat16),
            jax.ShapeDtypeStruct((tokens, 1), jnp.float32),
        ],
        compiler_params=pltpu.CompilerParams(vmem_limit_bytes=PACK_VMEM),
        cost_estimate=pl.CostEstimate(
            flops=4 * tokens * features, bytes_accessed=4 * tokens * features, transcendentals=tokens
        ),
        name="pack_hidden",
    )(hidden, gain)


NEAR = (0, -4, 4, 8)
HELD = (0, -1, 1, None)


def project_kernel(place_ref, tokens_ref, *refs):
    held_refs, (out_ref, weight) = refs[: len(HELD)], refs[len(HELD) :]

    @pl.when(pl.program_id(0) == 0)
    def _():
        here = place_ref[0]
        for held_ref, offset in zip(held_refs, HELD, strict=True):
            if offset is None:
                offset = jnp.where(lax.rem(here, 2) == 0, -2, 2)
            for at, further in enumerate(NEAR):
                plane = lax.rem(here + offset + further + PLANES, PLANES)
                rows = pl.ds(pl.multiple_of(plane * 64, 64), 64)
                weight[rows, :] = held_ref[at * 64 : at * 64 + 64, :]

    tokens = tokens_ref[...].reshape(-1, tokens_ref.shape[-1])
    product = jnp.dot(tokens, weight[...], preferred_element_type=jnp.float32)
    out_ref[...] = product.astype(jnp.bfloat16).reshape(out_ref.shape)


def project(place, tokens, held):
    peers, rows, features = tokens.shape
    width = held[0].shape[1]
    whole = [pl.BlockSpec(part.shape, lambda i, place: (0, 0)) for part in held]
    return pl.pallas_call(
        project_kernel,
        grid_spec=pltpu.PrefetchScalarGridSpec(
            num_scalar_prefetch=1,
            grid=(peers // SOURCES,),
            in_specs=[pl.BlockSpec((SOURCES, rows, features), lambda i, place: (i, 0, 0)), *whole],
            out_specs=pl.BlockSpec((SOURCES, rows, width), lambda i, place: (i, 0, 0)),
            scratch_shapes=[pltpu.VMEM((features, width), jnp.bfloat16)],
        ),
        out_shape=jax.ShapeDtypeStruct((peers, rows, width), jnp.bfloat16),
        compiler_params=pltpu.CompilerParams(vmem_limit_bytes=PROJECT_VMEM),
        cost_estimate=pl.CostEstimate(
            flops=2 * peers * rows * features * width,
            bytes_accessed=2 * (peers * rows * (features + width) + features * width),
            transcendentals=0,
        ),
        name="project_keys",
    )(place, tokens, *held)


def moved(block, target):
    return lax.ppermute(block, Z, [(z, target(z) % PLANES) for z in range(PLANES)])


def shards(
    hidden_in, norm_gain, key_weight, fragment_index, outer_params, outer_moment, inner_params
):
    replicas = 4
    block = key_weight[0]
    below, above = moved(block, lambda z: z + 4), moved(block, lambda z: z - 4)
    packed, scale = pack(hidden_in[0], norm_gain[None])
    packed, below, above, later = lax.optimization_barrier((packed, below, above, block))
    tokens = lax.all_to_all(packed, PLANE, 0, 0, tiled=True)
    across = moved(later, lambda z: z + 8)
    own = jnp.concatenate([block, below, above, across], axis=0)
    held = (
        own,
        moved(own, lambda z: z + 1),
        moved(own, lambda z: z - 1),
        moved(own, lambda z: z + 2 if z % 2 == 0 else z - 2),
    )
    place = lax.axis_index(Z).astype(jnp.int32)[None]
    partial = project(place, tokens, held)
    partial, fragment_index = lax.optimization_barrier((partial, fragment_index))
    partial = lax.all_to_all(partial, PLANE, 0, 0, tiled=True)
    layer_idx = fragment_index[0]
    outer_layer = lax.dynamic_index_in_dim(outer_params, layer_idx, 0, keepdims=False)
    moment_layer = lax.dynamic_index_in_dim(outer_moment, layer_idx, 0, keepdims=False)
    inner_layer = lax.dynamic_index_in_dim(inner_params[0], layer_idx, 0, keepdims=False)
    pseudo_grad = (outer_layer - inner_layer.astype(jnp.float32)).astype(jnp.bfloat16)
    every = lax.all_gather(pseudo_grad, REP, axis=0, tiled=False)
    summed = jnp.sum(every.astype(jnp.float32), axis=0)
    new_outer, new_moment = outer_update(summed / replicas, outer_layer, moment_layer)
    mixed_inner = (
        mix_keep * inner_layer.astype(jnp.float32) + (1.0 - mix_keep) * new_outer
    ).astype(jnp.bfloat16)
    keys = (jnp.sum(partial.astype(jnp.float32), axis=0) * scale).astype(jnp.bfloat16)
    return (keys[None], new_outer, new_moment, mixed_inner[None])


def solution(mesh):
    fine = Mesh(mesh.devices.reshape(2, 2, 16, 2, 4), ("yl", "core", "z", "yh", "x"))
    fsdp = ("z", "yh", "x")
    placed = (
        P(REP, fsdp, None),
        P(),
        P(REP, fsdp, None),
        P(),
        P(None, fsdp, None),
        P(None, fsdp, None),
        P(REP, None, fsdp, None),
    )
    return jax.shard_map(
        shards,
        mesh=fine,
        in_specs=placed,
        out_specs=(
            P(REP, fsdp, None),
            P(fsdp, None),
            P(fsdp, None),
            P(REP, fsdp, None),
        ),
        check_vma=False,
    )
```

```python
import jax
import jax.numpy as jnp
from jax import lax
from jax.experimental import pallas as pl
from jax.experimental.pallas import tpu as pltpu
from jax.sharding import Mesh, PartitionSpec as P

momentum_coef = 0.9
outer_rate = 0.7
mix_keep = 0.5
epsilon = 1e-05

Z, PLANE, REP = "z", ("yh", "x"), ("yl", "core")
PLANES, PEERS = 16, 8
ROWS, SOURCES = 64, 4
KERNEL_VMEM = 24 * 1024 * 1024


def outer_update(averaged, outer_layer, moment_layer):
    new_moment = momentum_coef * moment_layer + averaged
    new_outer = outer_layer - outer_rate * (averaged + momentum_coef * new_moment)
    return (new_outer, new_moment)


def pack_kernel(hidden_ref, gain_ref, packed_ref, scale_ref):
    hidden = hidden_ref[...].astype(jnp.float32)
    features = hidden.shape[1]
    mean_square = jnp.sum(hidden * hidden, axis=-1, keepdims=True) / features
    scale_ref[...] = lax.rsqrt(mean_square + epsilon)
    gained = hidden * gain_ref[...]
    low = lax.broadcasted_iota(jnp.int32, (hidden.shape[0], 128), 1) < 64
    for pair in range(PLANES // 2):
        for tile in range(PEERS // 2):
            start = pair * 1024 + tile * 128
            first = gained[:, start : start + 128]
            second = gained[:, start + 512 : start + 640]
            columns = slice(pair * 128, pair * 128 + 128)
            even = jnp.where(low, first, pltpu.roll(second, 64, 1))
            odd = jnp.where(low, pltpu.roll(first, 64, 1), second)
            packed_ref[2 * tile, :, columns] = even.astype(jnp.bfloat16)
            packed_ref[2 * tile + 1, :, columns] = odd.astype(jnp.bfloat16)


def pack(hidden, gain):
    tokens, features = hidden.shape
    return pl.pallas_call(
        pack_kernel,
        grid=(tokens // ROWS,),
        in_specs=[
            pl.BlockSpec((ROWS, features), lambda i: (i, 0)),
            pl.BlockSpec((1, features), lambda i: (0, 0)),
        ],
        out_specs=[
            pl.BlockSpec((PEERS, ROWS, features // PEERS), lambda i: (0, i, 0)),
            pl.BlockSpec((ROWS, 1), lambda i: (i, 0)),
        ],
        out_shape=[
            pltpu.HBM((PEERS, tokens, features // PEERS), jnp.bfloat16),
            jax.ShapeDtypeStruct((tokens, 1), jnp.float32),
        ],
        compiler_params=pltpu.CompilerParams(vmem_limit_bytes=KERNEL_VMEM),
        cost_estimate=pl.CostEstimate(
            flops=4 * tokens * features, bytes_accessed=4 * tokens * features, transcendentals=tokens
        ),
        name="pack_hidden",
    )(hidden, gain)


NEAR = (0, -4, 4, 8)
HELD = (0, -1, 1, None)


def project_kernel(place_ref, tokens_ref, *refs):
    held_refs, (out_ref, weight) = refs[: len(HELD)], refs[len(HELD) :]

    @pl.when(pl.program_id(0) == 0)
    def _():
        here = place_ref[0]
        for held_ref, offset in zip(held_refs, HELD, strict=True):
            if offset is None:
                offset = jnp.where(lax.rem(here, 2) == 0, -2, 2)
            for at, further in enumerate(NEAR):
                plane = lax.rem(here + offset + further + PLANES, PLANES)
                rows = pl.ds(pl.multiple_of(plane * 64, 64), 64)
                weight[rows, :] = held_ref[at * 64 : at * 64 + 64, :]

    tokens = tokens_ref[...].reshape(-1, tokens_ref.shape[-1])
    product = jnp.dot(tokens, weight[...], preferred_element_type=jnp.float32)
    out_ref[...] = product.astype(jnp.bfloat16).reshape(out_ref.shape)


def project(place, tokens, held):
    peers, rows, features = tokens.shape
    width = held[0].shape[1]
    whole = [pl.BlockSpec(part.shape, lambda i, place: (0, 0)) for part in held]
    return pl.pallas_call(
        project_kernel,
        grid_spec=pltpu.PrefetchScalarGridSpec(
            num_scalar_prefetch=1,
            grid=(peers // SOURCES,),
            in_specs=[pl.BlockSpec((SOURCES, rows, features), lambda i, place: (i, 0, 0)), *whole],
            out_specs=pl.BlockSpec((SOURCES, rows, width), lambda i, place: (i, 0, 0)),
            scratch_shapes=[pltpu.VMEM((features, width), jnp.bfloat16)],
        ),
        out_shape=pltpu.HBM((peers, rows, width), jnp.bfloat16),
        compiler_params=pltpu.CompilerParams(vmem_limit_bytes=KERNEL_VMEM),
        cost_estimate=pl.CostEstimate(
            flops=2 * peers * rows * features * width,
            bytes_accessed=2 * (peers * rows * (features + width) + features * width),
            transcendentals=0,
        ),
        name="project_keys",
    )(place, tokens, *held)


def moved(block, target):
    return lax.ppermute(block, Z, [(z, target(z) % PLANES) for z in range(PLANES)])


def shards(
    hidden_in, norm_gain, key_weight, fragment_index, outer_params, outer_moment, inner_params
):
    replicas = 4
    packed, scale = pack(hidden_in[0], norm_gain[None])
    packed, block = lax.optimization_barrier((packed, key_weight[0]))
    tokens = lax.all_to_all(packed, PLANE, 0, 0, tiled=True)
    below, above = moved(block, lambda z: z + 4), moved(block, lambda z: z - 4)
    across = moved(block, lambda z: z + 8)
    own = jnp.concatenate([block, below, above, across], axis=0)
    held = (
        own,
        moved(own, lambda z: z + 1),
        moved(own, lambda z: z - 1),
        moved(own, lambda z: z + 2 if z % 2 == 0 else z - 2),
    )
    place = lax.axis_index(Z).astype(jnp.int32)[None]
    partial = project(place, tokens, held)
    partial, fragment_index = lax.optimization_barrier((partial, fragment_index))
    partial = lax.all_to_all(partial, PLANE, 0, 0, tiled=True)
    layer_idx = fragment_index[0]
    outer_layer = lax.dynamic_index_in_dim(outer_params, layer_idx, 0, keepdims=False)
    moment_layer = lax.dynamic_index_in_dim(outer_moment, layer_idx, 0, keepdims=False)
    inner_layer = lax.dynamic_index_in_dim(inner_params[0], layer_idx, 0, keepdims=False)
    pseudo_grad = (outer_layer - inner_layer.astype(jnp.float32)).astype(jnp.bfloat16)
    summed = pseudo_grad.astype(jnp.float32)
    for other in range(1, replicas):
        pairs = [(replica, replica ^ other) for replica in range(replicas)]
        summed += lax.ppermute(pseudo_grad, REP, pairs).astype(jnp.float32)
    new_outer, new_moment = outer_update(summed / replicas, outer_layer, moment_layer)
    mixed_inner = (
        mix_keep * inner_layer.astype(jnp.float32) + (1.0 - mix_keep) * new_outer
    ).astype(jnp.bfloat16)
    keys = (jnp.sum(partial.astype(jnp.float32), axis=0) * scale).astype(jnp.bfloat16)
    return (keys[None], new_outer, new_moment, mixed_inner[None])


def solution(mesh):
    fine = Mesh(mesh.devices.reshape(2, 2, 16, 2, 4), ("yl", "core", "z", "yh", "x"))
    fsdp = ("z", "yh", "x")
    placed = (
        P(REP, fsdp, None),
        P(),
        P(REP, fsdp, None),
        P(),
        P(None, fsdp, None),
        P(None, fsdp, None),
        P(REP, None, fsdp, None),
    )
    return jax.shard_map(
        shards,
        mesh=fine,
        in_specs=placed,
        out_specs=(
            P(REP, fsdp, None),
            P(fsdp, None),
            P(fsdp, None),
            P(REP, fsdp, None),
        ),
        check_vma=False,
    )
```

```python
import jax
import jax.numpy as jnp
from jax import lax
from jax.experimental import pallas as pl
from jax.experimental.pallas import tpu as pltpu
from jax.sharding import Mesh, PartitionSpec as P

momentum_coef = 0.9
outer_rate = 0.7
mix_keep = 0.5
epsilon = 1e-05

Z, PLANE, REP = ("zh", "zl"), ("yh", "x"), ("yl", "core")
PLANES, PEERS = 16, 8
ROWS, SOURCES = 64, 4
KERNEL_VMEM = 24 * 1024 * 1024


def outer_update(averaged, outer_layer, moment_layer):
    new_moment = momentum_coef * moment_layer + averaged
    new_outer = outer_layer - outer_rate * (averaged + momentum_coef * new_moment)
    return (new_outer, new_moment)


def pack_kernel(hidden_ref, gain_ref, packed_ref, scale_ref):
    hidden = hidden_ref[...].astype(jnp.float32)
    features = hidden.shape[1]
    mean_square = jnp.sum(hidden * hidden, axis=-1, keepdims=True) / features
    scale_ref[...] = lax.rsqrt(mean_square + epsilon)
    gained = hidden * gain_ref[...]
    low = lax.broadcasted_iota(jnp.int32, (hidden.shape[0], 128), 1) < 64
    for pair in range(PLANES // 2):
        for tile in range(PEERS // 2):
            start = pair * 1024 + tile * 128
            first = gained[:, start : start + 128]
            second = gained[:, start + 512 : start + 640]
            columns = slice(pair * 128, pair * 128 + 128)
            even = jnp.where(low, first, pltpu.roll(second, 64, 1))
            odd = jnp.where(low, pltpu.roll(first, 64, 1), second)
            packed_ref[2 * tile, :, columns] = even.astype(jnp.bfloat16)
            packed_ref[2 * tile + 1, :, columns] = odd.astype(jnp.bfloat16)


def pack(hidden, gain):
    tokens, features = hidden.shape
    return pl.pallas_call(
        pack_kernel,
        grid=(tokens // ROWS,),
        in_specs=[
            pl.BlockSpec((ROWS, features), lambda i: (i, 0)),
            pl.BlockSpec((1, features), lambda i: (0, 0)),
        ],
        out_specs=[
            pl.BlockSpec((PEERS, ROWS, features // PEERS), lambda i: (0, i, 0)),
            pl.BlockSpec((ROWS, 1), lambda i: (i, 0)),
        ],
        out_shape=[
            pltpu.HBM((PEERS, tokens, features // PEERS), jnp.bfloat16),
            jax.ShapeDtypeStruct((tokens, 1), jnp.float32),
        ],
        compiler_params=pltpu.CompilerParams(vmem_limit_bytes=KERNEL_VMEM),
        cost_estimate=pl.CostEstimate(
            flops=4 * tokens * features, bytes_accessed=4 * tokens * features, transcendentals=tokens
        ),
        name="pack_hidden",
    )(hidden, gain)


HALF = PLANES // 2


def project_kernel(parity_ref, tokens_ref, own_ref, first_ref, second_ref, out_ref, weight):
    @pl.when(pl.program_id(0) == 0)
    def _():
        same = parity_ref[0]
        for at in range(HALF):
            other_ref, row = (first_ref, at) if at < HALF // 2 else (second_ref, at - HALF // 2)
            mine = pl.ds(pl.multiple_of((2 * at + same) * 64, 64), 64)
            weight[mine, :] = own_ref[at * 64 : at * 64 + 64, :]
            others = pl.ds(pl.multiple_of((2 * at + 1 - same) * 64, 64), 64)
            weight[others, :] = other_ref[row * 64 : row * 64 + 64, :]

    tokens = tokens_ref[...].reshape(-1, tokens_ref.shape[-1])
    product = jnp.dot(tokens, weight[...], preferred_element_type=jnp.float32)
    out_ref[...] = product.astype(jnp.bfloat16).reshape(out_ref.shape)


def project(parity, tokens, held):
    peers, rows, features = tokens.shape
    width = held[0].shape[1]
    whole = [pl.BlockSpec(part.shape, lambda i, parity: (0, 0)) for part in held]
    return pl.pallas_call(
        project_kernel,
        grid_spec=pltpu.PrefetchScalarGridSpec(
            num_scalar_prefetch=1,
            grid=(peers // SOURCES,),
            in_specs=[pl.BlockSpec((SOURCES, rows, features), lambda i, parity: (i, 0, 0)), *whole],
            out_specs=pl.BlockSpec((SOURCES, rows, width), lambda i, parity: (i, 0, 0)),
            scratch_shapes=[pltpu.VMEM((features, width), jnp.bfloat16)],
        ),
        out_shape=pltpu.HBM((peers, rows, width), jnp.bfloat16),
        compiler_params=pltpu.CompilerParams(vmem_limit_bytes=KERNEL_VMEM),
        cost_estimate=pl.CostEstimate(
            flops=2 * peers * rows * features * width,
            bytes_accessed=2 * (peers * rows * (features + width) + features * width),
            transcendentals=0,
        ),
        name="project_keys",
    )(parity, tokens, *held)


def moved(block, target):
    return lax.ppermute(block, Z, [(z, target(z) % PLANES) for z in range(PLANES)])


def shards(
    hidden_in, norm_gain, key_weight, fragment_index, outer_params, outer_moment, inner_params
):
    replicas = 4
    packed, scale = pack(hidden_in[0], norm_gain[None])
    packed, block = lax.optimization_barrier((packed, key_weight[0]))
    tokens = lax.all_to_all(packed, PLANE, 0, 0, tiled=True)
    own = lax.all_gather(block, "zh", axis=0, tiled=True)
    middle = own.shape[0] // 2
    first, second = moved(own[:middle], lambda z: z + 1), moved(own[middle:], lambda z: z - 1)
    parity = lax.axis_index("zl").astype(jnp.int32)[None]
    partial = project(parity, tokens, (own, first, second))
    partial, fragment_index = lax.optimization_barrier((partial, fragment_index))
    partial = lax.all_to_all(partial, PLANE, 0, 0, tiled=True)
    layer_idx = fragment_index[0]
    outer_layer = lax.dynamic_index_in_dim(outer_params, layer_idx, 0, keepdims=False)
    moment_layer = lax.dynamic_index_in_dim(outer_moment, layer_idx, 0, keepdims=False)
    inner_layer = lax.dynamic_index_in_dim(inner_params[0], layer_idx, 0, keepdims=False)
    pseudo_grad = (outer_layer - inner_layer.astype(jnp.float32)).astype(jnp.bfloat16)
    summed = pseudo_grad.astype(jnp.float32)
    for other in range(1, replicas):
        pairs = [(replica, replica ^ other) for replica in range(replicas)]
        summed += lax.ppermute(pseudo_grad, REP, pairs).astype(jnp.float32)
    new_outer, new_moment = outer_update(summed / replicas, outer_layer, moment_layer)
    mixed_inner = (
        mix_keep * inner_layer.astype(jnp.float32) + (1.0 - mix_keep) * new_outer
    ).astype(jnp.bfloat16)
    keys = (jnp.sum(partial.astype(jnp.float32), axis=0) * scale).astype(jnp.bfloat16)
    return (keys[None], new_outer, new_moment, mixed_inner[None])


def solution(mesh):
    fine = Mesh(mesh.devices.reshape(2, 2, 8, 2, 2, 4), ("yl", "core", "zh", "zl", "yh", "x"))
    fsdp = ("zh", "zl", "yh", "x")
    placed = (
        P(REP, fsdp, None),
        P(),
        P(REP, fsdp, None),
        P(),
        P(None, fsdp, None),
        P(None, fsdp, None),
        P(REP, None, fsdp, None),
    )
    return jax.shard_map(
        shards,
        mesh=fine,
        in_specs=placed,
        out_specs=(
            P(REP, fsdp, None),
            P(fsdp, None),
            P(fsdp, None),
            P(REP, fsdp, None),
        ),
        check_vma=False,
    )
```

```python
import jax
import jax.numpy as jnp
from jax import lax
from jax.experimental import pallas as pl
from jax.experimental.pallas import tpu as pltpu
from jax.sharding import Mesh, PartitionSpec as P

momentum_coef = 0.9
outer_rate = 0.7
mix_keep = 0.5
epsilon = 1e-05

Z, PLANE, REP = ("zh", "zl"), ("yh", "x"), ("yl", "core")
PLANES, PEERS = 16, 8
ROWS, SOURCES = 64, 4
KERNEL_VMEM = 24 * 1024 * 1024


def outer_update(averaged, outer_layer, moment_layer):
    new_moment = momentum_coef * moment_layer + averaged
    new_outer = outer_layer - outer_rate * (averaged + momentum_coef * new_moment)
    return (new_outer, new_moment)


def pack_kernel(hidden_ref, gain_ref, packed_ref, scale_ref):
    hidden = hidden_ref[...].astype(jnp.float32)
    features = hidden.shape[1]
    mean_square = jnp.sum(hidden * hidden, axis=-1, keepdims=True) / features
    scale_ref[...] = lax.rsqrt(mean_square + epsilon)
    gained = hidden * gain_ref[...]
    low = lax.broadcasted_iota(jnp.int32, (hidden.shape[0], 128), 1) < 64
    for pair in range(PLANES // 2):
        for tile in range(PEERS // 2):
            start = pair * 1024 + tile * 128
            first = gained[:, start : start + 128]
            second = gained[:, start + 512 : start + 640]
            columns = slice(pair * 128, pair * 128 + 128)
            even = jnp.where(low, first, pltpu.roll(second, 64, 1))
            odd = jnp.where(low, pltpu.roll(first, 64, 1), second)
            packed_ref[2 * tile, :, columns] = even.astype(jnp.bfloat16)
            packed_ref[2 * tile + 1, :, columns] = odd.astype(jnp.bfloat16)


def pack(hidden, gain):
    tokens, features = hidden.shape
    return pl.pallas_call(
        pack_kernel,
        grid=(tokens // ROWS,),
        in_specs=[
            pl.BlockSpec((ROWS, features), lambda i: (i, 0)),
            pl.BlockSpec((1, features), lambda i: (0, 0)),
        ],
        out_specs=[
            pl.BlockSpec((PEERS, ROWS, features // PEERS), lambda i: (0, i, 0)),
            pl.BlockSpec((ROWS, 1), lambda i: (i, 0)),
        ],
        out_shape=[
            pltpu.HBM((PEERS, tokens, features // PEERS), jnp.bfloat16),
            jax.ShapeDtypeStruct((tokens, 1), jnp.float32),
        ],
        compiler_params=pltpu.CompilerParams(vmem_limit_bytes=KERNEL_VMEM),
        cost_estimate=pl.CostEstimate(
            flops=4 * tokens * features, bytes_accessed=4 * tokens * features, transcendentals=tokens
        ),
        name="pack_hidden",
    )(hidden, gain)


STEPS = 4
HELD = (0, -1, 1, 2)


def project_kernel(residue_ref, tokens_ref, *refs):
    held_refs, (out_ref, weight) = refs[: len(HELD)], refs[len(HELD) :]

    @pl.when(pl.program_id(0) == 0)
    def _():
        for held_ref, above in zip(held_refs, HELD, strict=True):
            residue = lax.rem(residue_ref[0] + above + STEPS, STEPS)
            for at in range(PLANES // STEPS):
                rows = pl.ds(pl.multiple_of((at * STEPS + residue) * 64, 64), 64)
                weight[rows, :] = held_ref[at * 64 : at * 64 + 64, :]

    tokens = tokens_ref[...].reshape(-1, tokens_ref.shape[-1])
    product = jnp.dot(tokens, weight[...], preferred_element_type=jnp.float32)
    out_ref[...] = product.astype(jnp.bfloat16).reshape(out_ref.shape)


def project(residue, tokens, held):
    peers, rows, features = tokens.shape
    width = held[0].shape[1]
    whole = [pl.BlockSpec(part.shape, lambda i, residue: (0, 0)) for part in held]
    return pl.pallas_call(
        project_kernel,
        grid_spec=pltpu.PrefetchScalarGridSpec(
            num_scalar_prefetch=1,
            grid=(peers // SOURCES,),
            in_specs=[pl.BlockSpec((SOURCES, rows, features), lambda i, residue: (i, 0, 0)), *whole],
            out_specs=pl.BlockSpec((SOURCES, rows, width), lambda i, residue: (i, 0, 0)),
            scratch_shapes=[pltpu.VMEM((features, width), jnp.bfloat16)],
        ),
        out_shape=pltpu.HBM((peers, rows, width), jnp.bfloat16),
        compiler_params=pltpu.CompilerParams(vmem_limit_bytes=KERNEL_VMEM),
        cost_estimate=pl.CostEstimate(
            flops=2 * peers * rows * features * width,
            bytes_accessed=2 * (peers * rows * (features + width) + features * width),
            transcendentals=0,
        ),
        name="project_keys",
    )(residue, tokens, *held)


def moved(block, target):
    return lax.ppermute(block, Z, [(z, target(z) % PLANES) for z in range(PLANES)])


def shards(
    hidden_in, norm_gain, key_weight, fragment_index, outer_params, outer_moment, inner_params
):
    replicas = 4
    packed, scale = pack(hidden_in[0], norm_gain[None])
    packed, block = lax.optimization_barrier((packed, key_weight[0]))
    tokens = lax.all_to_all(packed, PLANE, 0, 0, tiled=True)
    own = lax.all_gather(block, "zh", axis=0, tiled=True)
    held = (
        own,
        moved(own, lambda z: z + 1),
        moved(own, lambda z: z - 1),
        moved(own, lambda z: z + 2 if z % 2 == 0 else z - 2),
    )
    residue = lax.axis_index("zl").astype(jnp.int32)[None]
    partial = project(residue, tokens, held)
    partial, fragment_index = lax.optimization_barrier((partial, fragment_index))
    partial = lax.all_to_all(partial, PLANE, 0, 0, tiled=True)
    layer_idx = fragment_index[0]
    outer_layer = lax.dynamic_index_in_dim(outer_params, layer_idx, 0, keepdims=False)
    moment_layer = lax.dynamic_index_in_dim(outer_moment, layer_idx, 0, keepdims=False)
    inner_layer = lax.dynamic_index_in_dim(inner_params[0], layer_idx, 0, keepdims=False)
    pseudo_grad = (outer_layer - inner_layer.astype(jnp.float32)).astype(jnp.bfloat16)
    summed = pseudo_grad.astype(jnp.float32)
    for other in range(1, replicas):
        pairs = [(replica, replica ^ other) for replica in range(replicas)]
        summed += lax.ppermute(pseudo_grad, REP, pairs).astype(jnp.float32)
    new_outer, new_moment = outer_update(summed / replicas, outer_layer, moment_layer)
    mixed_inner = (
        mix_keep * inner_layer.astype(jnp.float32) + (1.0 - mix_keep) * new_outer
    ).astype(jnp.bfloat16)
    keys = (jnp.sum(partial.astype(jnp.float32), axis=0) * scale).astype(jnp.bfloat16)
    return (keys[None], new_outer, new_moment, mixed_inner[None])


def solution(mesh):
    fine = Mesh(mesh.devices.reshape(2, 2, 4, 4, 2, 4), ("yl", "core", "zh", "zl", "yh", "x"))
    fsdp = ("zh", "zl", "yh", "x")
    placed = (
        P(REP, fsdp, None),
        P(),
        P(REP, fsdp, None),
        P(),
        P(None, fsdp, None),
        P(None, fsdp, None),
        P(REP, None, fsdp, None),
    )
    return jax.shard_map(
        shards,
        mesh=fine,
        in_specs=placed,
        out_specs=(
            P(REP, fsdp, None),
            P(fsdp, None),
            P(fsdp, None),
            P(REP, fsdp, None),
        ),
        check_vma=False,
    )
```

```python
import jax
import jax.numpy as jnp
from jax import lax
from jax.experimental import pallas as pl
from jax.experimental.pallas import tpu as pltpu
from jax.sharding import Mesh, PartitionSpec as P

momentum_coef = 0.9
outer_rate = 0.7
mix_keep = 0.5
epsilon = 1e-05

Z, PLANE, REP = ("zh", "zl"), ("yh", "x"), ("yl", "core")
PLANES, PEERS = 16, 8
ROWS, SOURCES = 64, 4
KERNEL_VMEM = 24 * 1024 * 1024


def outer_update(averaged, outer_layer, moment_layer):
    new_moment = momentum_coef * moment_layer + averaged
    new_outer = outer_layer - outer_rate * (averaged + momentum_coef * new_moment)
    return (new_outer, new_moment)


def pack_kernel(hidden_ref, gain_ref, packed_ref, scale_ref):
    hidden = hidden_ref[...].astype(jnp.float32)
    features = hidden.shape[1]
    mean_square = jnp.sum(hidden * hidden, axis=-1, keepdims=True) / features
    scale_ref[...] = lax.rsqrt(mean_square + epsilon)
    gained = hidden * gain_ref[...]
    low = lax.broadcasted_iota(jnp.int32, (hidden.shape[0], 128), 1) < 64
    for pair in range(PLANES // 2):
        for tile in range(PEERS // 2):
            start = pair * 1024 + tile * 128
            first = gained[:, start : start + 128]
            second = gained[:, start + 512 : start + 640]
            columns = slice(pair * 128, pair * 128 + 128)
            even = jnp.where(low, first, pltpu.roll(second, 64, 1))
            odd = jnp.where(low, pltpu.roll(first, 64, 1), second)
            packed_ref[2 * tile, :, columns] = even.astype(jnp.bfloat16)
            packed_ref[2 * tile + 1, :, columns] = odd.astype(jnp.bfloat16)


def pack(hidden, gain):
    tokens, features = hidden.shape
    return pl.pallas_call(
        pack_kernel,
        grid=(tokens // ROWS,),
        in_specs=[
            pl.BlockSpec((ROWS, features), lambda i: (i, 0)),
            pl.BlockSpec((1, features), lambda i: (0, 0)),
        ],
        out_specs=[
            pl.BlockSpec((PEERS, ROWS, features // PEERS), lambda i: (0, i, 0)),
            pl.BlockSpec((ROWS, 1), lambda i: (i, 0)),
        ],
        out_shape=[
            pltpu.HBM((PEERS, tokens, features // PEERS), jnp.bfloat16),
            jax.ShapeDtypeStruct((tokens, 1), jnp.float32),
        ],
        compiler_params=pltpu.CompilerParams(vmem_limit_bytes=KERNEL_VMEM),
        cost_estimate=pl.CostEstimate(
            flops=4 * tokens * features, bytes_accessed=4 * tokens * features, transcendentals=tokens
        ),
        name="pack_hidden",
    )(hidden, gain)


STEPS = 4
HELD = (0, -1, 1, 2)


def project_kernel(residue_ref, tokens_ref, *refs):
    held_refs, (out_ref, weight) = refs[: len(HELD)], refs[len(HELD) :]

    @pl.when(pl.program_id(0) == 0)
    def _():
        for held_ref, above in zip(held_refs, HELD, strict=True):
            residue = lax.rem(residue_ref[0] + above + STEPS, STEPS)
            for at in range(PLANES // STEPS):
                rows = pl.ds(pl.multiple_of((at * STEPS + residue) * 64, 64), 64)
                weight[rows, :] = held_ref[at * 64 : at * 64 + 64, :]

    tokens = tokens_ref[...].reshape(-1, tokens_ref.shape[-1])
    product = jnp.dot(tokens, weight[...], preferred_element_type=jnp.float32)
    out_ref[...] = product.astype(jnp.bfloat16).reshape(out_ref.shape)


def project(residue, tokens, held):
    peers, rows, features = tokens.shape
    width = held[0].shape[1]
    whole = [pl.BlockSpec(part.shape, lambda i, residue: (0, 0)) for part in held]
    return pl.pallas_call(
        project_kernel,
        grid_spec=pltpu.PrefetchScalarGridSpec(
            num_scalar_prefetch=1,
            grid=(peers // SOURCES,),
            in_specs=[pl.BlockSpec((SOURCES, rows, features), lambda i, residue: (i, 0, 0)), *whole],
            out_specs=pl.BlockSpec((SOURCES, rows, width), lambda i, residue: (i, 0, 0)),
            scratch_shapes=[pltpu.VMEM((features, width), jnp.bfloat16)],
        ),
        out_shape=pltpu.HBM((peers, rows, width), jnp.bfloat16),
        compiler_params=pltpu.CompilerParams(vmem_limit_bytes=KERNEL_VMEM),
        cost_estimate=pl.CostEstimate(
            flops=2 * peers * rows * features * width,
            bytes_accessed=2 * (peers * rows * (features + width) + features * width),
            transcendentals=0,
        ),
        name="project_keys",
    )(residue, tokens, *held)


def moved(block, target):
    return lax.ppermute(block, Z, [(z, target(z) % PLANES) for z in range(PLANES)])


def shards(
    hidden_in, norm_gain, key_weight, fragment_index, outer_params, outer_moment, inner_params
):
    replicas = 4
    layer_idx = fragment_index[0]
    outer_layer = lax.dynamic_index_in_dim(outer_params, layer_idx, 0, keepdims=False)
    inner_layer = lax.dynamic_index_in_dim(inner_params[0], layer_idx, 0, keepdims=False)
    pseudo_grad = (outer_layer - inner_layer.astype(jnp.float32)).astype(jnp.bfloat16)

    packed, scale = pack(hidden_in[0], norm_gain[None])
    packed, block = lax.optimization_barrier((packed, key_weight[0]))
    tokens = lax.all_to_all(packed, PLANE, 0, 0, tiled=True)
    own = lax.all_gather(block, "zh", axis=0, tiled=True)
    own, pseudo_grad = lax.optimization_barrier((own, pseudo_grad))
    held = (
        own,
        moved(own, lambda z: z + 1),
        moved(own, lambda z: z - 1),
        moved(own, lambda z: z + 2 if z % 2 == 0 else z - 2),
    )
    others = []
    for other in range(1, replicas):
        pairs = [(replica, replica ^ other) for replica in range(replicas)]
        others.append(lax.ppermute(pseudo_grad, REP, pairs))
    residue = lax.axis_index("zl").astype(jnp.int32)[None]
    partial = project(residue, tokens, held)
    partial, layer_idx, others = lax.optimization_barrier((partial, layer_idx, others))
    partial = lax.all_to_all(partial, PLANE, 0, 0, tiled=True)
    outer_layer = lax.dynamic_index_in_dim(outer_params, layer_idx, 0, keepdims=False)
    moment_layer = lax.dynamic_index_in_dim(outer_moment, layer_idx, 0, keepdims=False)
    inner_layer = lax.dynamic_index_in_dim(inner_params[0], layer_idx, 0, keepdims=False)
    summed = pseudo_grad.astype(jnp.float32) + sum(part.astype(jnp.float32) for part in others)
    new_outer, new_moment = outer_update(summed / replicas, outer_layer, moment_layer)
    mixed_inner = (
        mix_keep * inner_layer.astype(jnp.float32) + (1.0 - mix_keep) * new_outer
    ).astype(jnp.bfloat16)
    keys = (jnp.sum(partial.astype(jnp.float32), axis=0) * scale).astype(jnp.bfloat16)
    return (keys[None], new_outer, new_moment, mixed_inner[None])


def solution(mesh):
    fine = Mesh(mesh.devices.reshape(2, 2, 4, 4, 2, 4), ("yl", "core", "zh", "zl", "yh", "x"))
    fsdp = ("zh", "zl", "yh", "x")
    placed = (
        P(REP, fsdp, None),
        P(),
        P(REP, fsdp, None),
        P(),
        P(None, fsdp, None),
        P(None, fsdp, None),
        P(REP, None, fsdp, None),
    )
    return jax.shard_map(
        shards,
        mesh=fine,
        in_specs=placed,
        out_specs=(
            P(REP, fsdp, None),
            P(fsdp, None),
            P(fsdp, None),
            P(REP, fsdp, None),
        ),
        check_vma=False,
    )
```

```python
import jax
import jax.numpy as jnp
from jax import lax
from jax.experimental import pallas as pl
from jax.experimental.pallas import tpu as pltpu
from jax.sharding import Mesh, PartitionSpec as P

momentum_coef = 0.9
outer_rate = 0.7
mix_keep = 0.5
epsilon = 1e-05

REP, LINE = ("yl", "core"), ("core", "zh", "zl", "yh", "x")
PLANES, SIDES, COLUMNS = 16, 2, 4
CLASSES, ROWS, SOURCES = 4, 64, 2
KERNEL_VMEM = 24 * 1024 * 1024


def place_of(core, z, yh, x):
    return ((core * PLANES + z % PLANES) * SIDES + yh) * COLUMNS + x


def class_of(core, z, x):
    along = x // 2 if core == 0 else int(x in (1, 2))
    return along + 2 * (z % 2)


def exchange_groups():
    groups = []
    for core in range(2):
        starts = range(core, PLANES, 2)
        pairs = ((0, 3), (1, 2)) if core == 0 else ((0, 1), (2, 3))
        for z in starts:
            for yh in range(SIDES):
                for pair in pairs:
                    members = [(core, at % PLANES, yh, x) for at in (z, z + 1) for x in pair]
                    members.sort(key=lambda m: class_of(m[0], m[1], m[3]))
                    groups.append([place_of(*m) for m in members])
    return groups


def flipped(block, across_x, across_y):
    pairs = []
    for core in range(2):
        for z in range(PLANES):
            for yh in range(SIDES):
                for x in range(COLUMNS):
                    other = x ^ (1 if core == 0 else 3) if across_x else x
                    pairs.append((place_of(core, z, yh, x), place_of(core, z, yh ^ across_y, other)))
    return lax.ppermute(block, LINE, pairs)


def outer_update(averaged, outer_layer, moment_layer):
    new_moment = momentum_coef * moment_layer + averaged
    new_outer = outer_layer - outer_rate * (averaged + momentum_coef * new_moment)
    return (new_outer, new_moment)


def pack_kernel(core_ref, hidden_ref, gain_ref, packed_ref, scale_ref):
    hidden = hidden_ref[...].astype(jnp.float32)
    features = hidden.shape[1]
    mean_square = jnp.sum(hidden * hidden, axis=-1, keepdims=True) / features
    scale_ref[...] = lax.rsqrt(mean_square + epsilon)
    gained = hidden * gain_ref[...]
    lane = lax.broadcasted_iota(jnp.int32, (hidden.shape[0], 128), 1)
    swapped = jnp.logical_and(lane >= 64, core_ref[0] == 1)
    for z in range(PLANES):
        for yh in range(SIDES):
            start = z * 512 + yh * 256
            first, second = gained[:, start : start + 128], gained[:, start + 128 : start + 256]
            place = ((z // 2) * SIDES + yh) * 128
            columns, parity = slice(place, place + 128), z % 2
            packed_ref[2 * parity, :, columns] = jnp.where(swapped, second, first).astype(jnp.bfloat16)
            packed_ref[2 * parity + 1, :, columns] = jnp.where(swapped, first, second).astype(
                jnp.bfloat16
            )


def pack(core, hidden, gain):
    tokens, features = hidden.shape
    return pl.pallas_call(
        pack_kernel,
        grid_spec=pltpu.PrefetchScalarGridSpec(
            num_scalar_prefetch=1,
            grid=(tokens // ROWS,),
            in_specs=[
                pl.BlockSpec((ROWS, features), lambda i, core: (i, 0)),
                pl.BlockSpec((1, features), lambda i, core: (0, 0)),
            ],
            out_specs=[
                pl.BlockSpec((CLASSES, ROWS, features // CLASSES), lambda i, core: (0, i, 0)),
                pl.BlockSpec((ROWS, 1), lambda i, core: (i, 0)),
            ],
        ),
        out_shape=[
            pltpu.HBM((CLASSES, tokens, features // CLASSES), jnp.bfloat16),
            jax.ShapeDtypeStruct((tokens, 1), jnp.float32),
        ],
        compiler_params=pltpu.CompilerParams(vmem_limit_bytes=KERNEL_VMEM),
        cost_estimate=pl.CostEstimate(
            flops=4 * tokens * features, bytes_accessed=4 * tokens * features, transcendentals=tokens
        ),
        name="pack_hidden",
    )(core, hidden, gain)


def project_kernel(place_ref, tokens_ref, own_ref, x_ref, y_ref, both_ref, out_ref, weight):
    @pl.when(pl.program_id(0) == 0)
    def _():
        side, half = place_ref[0], place_ref[1]
        held = ((own_ref, side, half), (x_ref, side, 1 - half), (y_ref, 1 - side, half), (both_ref, 1 - side, 1 - half))
        for held_ref, at_side, at_half in held:
            offset = at_side * 128 + at_half * 64
            for at in range(PLANES // 2):
                rows = pl.ds(pl.multiple_of(at * 256 + offset, 64), 64)
                weight[rows, :] = held_ref[at * 64 : at * 64 + 64, :]

    tokens = tokens_ref[...].reshape(-1, tokens_ref.shape[-1])
    product = jnp.dot(tokens, weight[...], preferred_element_type=jnp.float32)
    out_ref[...] = product.astype(jnp.bfloat16).reshape(out_ref.shape)


def project(place, tokens, held):
    sources, rows, features = tokens.shape
    width = held[0].shape[1]
    whole = [pl.BlockSpec(part.shape, lambda i, place: (0, 0)) for part in held]
    return pl.pallas_call(
        project_kernel,
        grid_spec=pltpu.PrefetchScalarGridSpec(
            num_scalar_prefetch=1,
            grid=(sources // SOURCES,),
            in_specs=[pl.BlockSpec((SOURCES, rows, features), lambda i, place: (i, 0, 0)), *whole],
            out_specs=pl.BlockSpec((SOURCES, rows, width), lambda i, place: (i, 0, 0)),
            scratch_shapes=[pltpu.VMEM((features, width), jnp.bfloat16)],
        ),
        out_shape=pltpu.HBM((sources, rows, width), jnp.bfloat16),
        compiler_params=pltpu.CompilerParams(vmem_limit_bytes=KERNEL_VMEM),
        cost_estimate=pl.CostEstimate(
            flops=2 * sources * rows * features * width,
            bytes_accessed=2 * (sources * rows * (features + width) + features * width),
            transcendentals=0,
        ),
        name="project_keys",
    )(place, tokens, *held)


def shards(
    hidden_in, norm_gain, key_weight, fragment_index, outer_params, outer_moment, inner_params
):
    replicas = 4
    layer_idx = fragment_index[0]
    outer_layer = lax.dynamic_index_in_dim(outer_params, layer_idx, 0, keepdims=False)
    inner_layer = lax.dynamic_index_in_dim(inner_params[0], layer_idx, 0, keepdims=False)
    pseudo_grad = (outer_layer - inner_layer.astype(jnp.float32)).astype(jnp.bfloat16)

    core, yh, x = (lax.axis_index(axis).astype(jnp.int32) for axis in ("core", "yh", "x"))
    own = lax.all_gather(key_weight[0], "zh", axis=0, tiled=True)
    own, gain = lax.optimization_barrier((own, norm_gain))
    packed, scale = pack(core[None], hidden_in[0], gain[None])
    packed, own, pseudo_grad = lax.optimization_barrier((packed, own, pseudo_grad))
    groups = exchange_groups()
    tokens = lax.all_to_all(packed, LINE, 0, 0, axis_index_groups=groups, tiled=True)
    held = (own, flipped(own, 1, 0), flipped(own, 0, 1), flipped(own, 1, 1))
    others = []
    for other in range(1, replicas):
        pairs = [(replica, replica ^ other) for replica in range(replicas)]
        others.append(lax.ppermute(pseudo_grad, REP, pairs))
    partial = project(jnp.stack([yh, lax.rem(x, 2)]), tokens, held)
    partial, layer_idx, others = lax.optimization_barrier((partial, layer_idx, others))
    partial = lax.all_to_all(partial, LINE, 0, 0, axis_index_groups=groups, tiled=True)
    outer_layer = lax.dynamic_index_in_dim(outer_params, layer_idx, 0, keepdims=False)
    moment_layer = lax.dynamic_index_in_dim(outer_moment, layer_idx, 0, keepdims=False)
    inner_layer = lax.dynamic_index_in_dim(inner_params[0], layer_idx, 0, keepdims=False)
    summed = pseudo_grad.astype(jnp.float32) + sum(part.astype(jnp.float32) for part in others)
    new_outer, new_moment = outer_update(summed / replicas, outer_layer, moment_layer)
    mixed_inner = (
        mix_keep * inner_layer.astype(jnp.float32) + (1.0 - mix_keep) * new_outer
    ).astype(jnp.bfloat16)
    keys = (jnp.sum(partial.astype(jnp.float32), axis=0) * scale).astype(jnp.bfloat16)
    return (keys[None], new_outer, new_moment, mixed_inner[None])


def solution(mesh):
    fine = Mesh(mesh.devices.reshape(2, 2, 8, 2, 2, 4), ("yl", "core", "zh", "zl", "yh", "x"))
    fsdp = ("zh", "zl", "yh", "x")
    placed = (
        P(REP, fsdp, None),
        P(),
        P(REP, fsdp, None),
        P(),
        P(None, fsdp, None),
        P(None, fsdp, None),
        P(REP, None, fsdp, None),
    )
    return jax.shard_map(
        shards,
        mesh=fine,
        in_specs=placed,
        out_specs=(
            P(REP, fsdp, None),
            P(fsdp, None),
            P(fsdp, None),
            P(REP, fsdp, None),
        ),
        check_vma=False,
    )
```

```python
import jax
import jax.numpy as jnp
from jax import lax
from jax.experimental import pallas as pl
from jax.experimental.pallas import tpu as pltpu
from jax.sharding import Mesh, PartitionSpec as P

momentum_coef = 0.9
outer_rate = 0.7
mix_keep = 0.5
epsilon = 1e-05

REP, LINE = ("yl", "core"), ("core", "zh", "zm", "zl", "yh", "x")
PLANES, SIDES, COLUMNS = 16, 2, 4
CLASSES, ROWS, SOURCES = 4, 64, 2
KERNEL_VMEM = 24 * 1024 * 1024


def place_of(core, z, yh, x):
    return ((core * PLANES + z % PLANES) * SIDES + yh) * COLUMNS + x


def class_of(core, z, x):
    along = x // 2 if core == 0 else int(x in (1, 2))
    return along + 2 * (z % 2)


def exchange_groups():
    groups = []
    for core in range(2):
        starts = range(core, PLANES, 2)
        pairs = ((0, 3), (1, 2)) if core == 0 else ((0, 1), (2, 3))
        for z in starts:
            for yh in range(SIDES):
                for pair in pairs:
                    members = [(core, at % PLANES, yh, x) for at in (z, z + 1) for x in pair]
                    members.sort(key=lambda m: class_of(m[0], m[1], m[3]))
                    groups.append([place_of(*m) for m in members])
    return groups


def flipped(block, across_x, across_y):
    pairs = []
    for core in range(2):
        for z in range(PLANES):
            for yh in range(SIDES):
                for x in range(COLUMNS):
                    other = x ^ (1 if core == 0 else 3) if across_x else x
                    pairs.append((place_of(core, z, yh, x), place_of(core, z, yh ^ across_y, other)))
    return lax.ppermute(block, LINE, pairs)


def outer_update(averaged, outer_layer, moment_layer):
    new_moment = momentum_coef * moment_layer + averaged
    new_outer = outer_layer - outer_rate * (averaged + momentum_coef * new_moment)
    return (new_outer, new_moment)


def pack_kernel(core_ref, hidden_ref, gain_ref, packed_ref, scale_ref):
    hidden = hidden_ref[...].astype(jnp.float32)
    features = hidden.shape[1]
    mean_square = jnp.sum(hidden * hidden, axis=-1, keepdims=True) / features
    scale_ref[...] = lax.rsqrt(mean_square + epsilon)
    gained = hidden * gain_ref[...]
    lane = lax.broadcasted_iota(jnp.int32, (hidden.shape[0], 128), 1)
    swapped = jnp.logical_and(lane >= 64, core_ref[0] == 1)
    for z in range(PLANES):
        for yh in range(SIDES):
            start = z * 512 + yh * 256
            first, second = gained[:, start : start + 128], gained[:, start + 128 : start + 256]
            place = ((z // 2) * SIDES + yh) * 128
            columns, parity = slice(place, place + 128), z % 2
            packed_ref[2 * parity, :, columns] = jnp.where(swapped, second, first).astype(jnp.bfloat16)
            packed_ref[2 * parity + 1, :, columns] = jnp.where(swapped, first, second).astype(
                jnp.bfloat16
            )


def pack(core, hidden, gain):
    tokens, features = hidden.shape
    return pl.pallas_call(
        pack_kernel,
        grid_spec=pltpu.PrefetchScalarGridSpec(
            num_scalar_prefetch=1,
            grid=(tokens // ROWS,),
            in_specs=[
                pl.BlockSpec((ROWS, features), lambda i, core: (i, 0)),
                pl.BlockSpec((1, features), lambda i, core: (0, 0)),
            ],
            out_specs=[
                pl.BlockSpec((CLASSES, ROWS, features // CLASSES), lambda i, core: (0, i, 0)),
                pl.BlockSpec((ROWS, 1), lambda i, core: (i, 0)),
            ],
        ),
        out_shape=[
            pltpu.HBM((CLASSES, tokens, features // CLASSES), jnp.bfloat16),
            jax.ShapeDtypeStruct((tokens, 1), jnp.float32),
        ],
        compiler_params=pltpu.CompilerParams(vmem_limit_bytes=KERNEL_VMEM),
        cost_estimate=pl.CostEstimate(
            flops=4 * tokens * features, bytes_accessed=4 * tokens * features, transcendentals=tokens
        ),
        name="pack_hidden",
    )(core, hidden, gain)


def project_kernel(place_ref, tokens_ref, own_ref, x_ref, y_ref, both_ref, out_ref, weight):
    @pl.when(pl.program_id(0) == 0)
    def _():
        side, half = place_ref[0], place_ref[1]
        held = ((own_ref, side, half), (x_ref, side, 1 - half), (y_ref, 1 - side, half), (both_ref, 1 - side, 1 - half))
        for held_ref, at_side, at_half in held:
            offset = at_side * 128 + at_half * 64
            for at in range(PLANES // 2):
                middle = place_ref[2] if at % 2 == 0 else 1 - place_ref[2]
                rows = pl.ds(pl.multiple_of((at // 2 * 2 + middle) * 256 + offset, 64), 64)
                weight[rows, :] = held_ref[at * 64 : at * 64 + 64, :]

    tokens = tokens_ref[...].reshape(-1, tokens_ref.shape[-1])
    product = jnp.dot(tokens, weight[...], preferred_element_type=jnp.float32)
    out_ref[...] = product.astype(jnp.bfloat16).reshape(out_ref.shape)


def project(place, tokens, held):
    sources, rows, features = tokens.shape
    width = held[0].shape[1]
    whole = [pl.BlockSpec(part.shape, lambda i, place: (0, 0)) for part in held]
    return pl.pallas_call(
        project_kernel,
        grid_spec=pltpu.PrefetchScalarGridSpec(
            num_scalar_prefetch=1,
            grid=(sources // SOURCES,),
            in_specs=[pl.BlockSpec((SOURCES, rows, features), lambda i, place: (i, 0, 0)), *whole],
            out_specs=pl.BlockSpec((SOURCES, rows, width), lambda i, place: (i, 0, 0)),
            scratch_shapes=[pltpu.VMEM((features, width), jnp.bfloat16)],
        ),
        out_shape=pltpu.HBM((sources, rows, width), jnp.bfloat16),
        compiler_params=pltpu.CompilerParams(vmem_limit_bytes=KERNEL_VMEM),
        cost_estimate=pl.CostEstimate(
            flops=2 * sources * rows * features * width,
            bytes_accessed=2 * (sources * rows * (features + width) + features * width),
            transcendentals=0,
        ),
        name="project_keys",
    )(place, tokens, *held)


def shards(
    hidden_in, norm_gain, key_weight, fragment_index, outer_params, outer_moment, inner_params
):
    replicas = 4
    layer_idx = fragment_index[0]
    outer_layer = lax.dynamic_index_in_dim(outer_params, layer_idx, 0, keepdims=False)
    inner_layer = lax.dynamic_index_in_dim(inner_params[0], layer_idx, 0, keepdims=False)
    pseudo_grad = (outer_layer - inner_layer.astype(jnp.float32)).astype(jnp.bfloat16)

    core, middle, yh, x = (lax.axis_index(axis).astype(jnp.int32) for axis in ("core", "zm", "yh", "x"))
    block = key_weight[0]
    block = jnp.concatenate([block, lax.ppermute(block, "zm", [(0, 1), (1, 0)])], axis=0)
    packed, scale = pack(core[None], hidden_in[0], norm_gain[None])
    packed, block, pseudo_grad = lax.optimization_barrier((packed, block, pseudo_grad))
    groups = exchange_groups()
    tokens = lax.all_to_all(packed, LINE, 0, 0, axis_index_groups=groups, tiled=True)
    own = lax.all_gather(block, "zh", axis=0, tiled=True)
    own, pseudo_grad = lax.optimization_barrier((own, pseudo_grad))
    held = (own, flipped(own, 1, 0), flipped(own, 0, 1), flipped(own, 1, 1))
    others = []
    for other in range(1, replicas):
        pairs = [(replica, replica ^ other) for replica in range(replicas)]
        others.append(lax.ppermute(pseudo_grad, REP, pairs))
    partial = project(jnp.stack([yh, lax.rem(x, 2), middle]), tokens, held)
    partial, layer_idx, others = lax.optimization_barrier((partial, layer_idx, others))
    partial = lax.all_to_all(partial, LINE, 0, 0, axis_index_groups=groups, tiled=True)
    outer_layer = lax.dynamic_index_in_dim(outer_params, layer_idx, 0, keepdims=False)
    moment_layer = lax.dynamic_index_in_dim(outer_moment, layer_idx, 0, keepdims=False)
    inner_layer = lax.dynamic_index_in_dim(inner_params[0], layer_idx, 0, keepdims=False)
    summed = pseudo_grad.astype(jnp.float32) + sum(part.astype(jnp.float32) for part in others)
    new_outer, new_moment = outer_update(summed / replicas, outer_layer, moment_layer)
    mixed_inner = (
        mix_keep * inner_layer.astype(jnp.float32) + (1.0 - mix_keep) * new_outer
    ).astype(jnp.bfloat16)
    keys = (jnp.sum(partial.astype(jnp.float32), axis=0) * scale).astype(jnp.bfloat16)
    return (keys[None], new_outer, new_moment, mixed_inner[None])


def solution(mesh):
    fine = Mesh(mesh.devices.reshape(2, 2, 4, 2, 2, 2, 4), ("yl", "core", "zh", "zm", "zl", "yh", "x"))
    fsdp = ("zh", "zm", "zl", "yh", "x")
    placed = (
        P(REP, fsdp, None),
        P(),
        P(REP, fsdp, None),
        P(),
        P(None, fsdp, None),
        P(None, fsdp, None),
        P(REP, None, fsdp, None),
    )
    return jax.shard_map(
        shards,
        mesh=fine,
        in_specs=placed,
        out_specs=(
            P(REP, fsdp, None),
            P(fsdp, None),
            P(fsdp, None),
            P(REP, fsdp, None),
        ),
        check_vma=False,
    )
```

```python
import jax
import jax.numpy as jnp
from jax import lax
from jax.experimental import pallas as pl
from jax.experimental.pallas import tpu as pltpu
from jax.sharding import Mesh, PartitionSpec as P

momentum_coef = 0.9
outer_rate = 0.7
mix_keep = 0.5
epsilon = 1e-05

Z, ROW, REP = ("zh", "zl"), "x", ("yl", "core")
PLANES, SIDES, PEERS = 16, 2, 4
ROWS, SOURCES = 64, 2
KERNEL_VMEM = 24 * 1024 * 1024


def outer_update(averaged, outer_layer, moment_layer):
    new_moment = momentum_coef * moment_layer + averaged
    new_outer = outer_layer - outer_rate * (averaged + momentum_coef * new_moment)
    return (new_outer, new_moment)


def pack_kernel(hidden_ref, gain_ref, packed_ref, scale_ref):
    hidden = hidden_ref[...].astype(jnp.float32)
    features = hidden.shape[1]
    mean_square = jnp.sum(hidden * hidden, axis=-1, keepdims=True) / features
    scale_ref[...] = lax.rsqrt(mean_square + epsilon)
    gained = hidden * gain_ref[...]
    low = lax.broadcasted_iota(jnp.int32, (hidden.shape[0], 128), 1) < 64
    for z in range(PLANES):
        for pair in range(PEERS // 2):
            start = z * 512 + pair * 128
            first, second = gained[:, start : start + 128], gained[:, start + 256 : start + 384]
            columns = slice(z * 128, z * 128 + 128)
            even = jnp.where(low, first, pltpu.roll(second, 64, 1))
            odd = jnp.where(low, pltpu.roll(first, 64, 1), second)
            packed_ref[2 * pair, :, columns] = even.astype(jnp.bfloat16)
            packed_ref[2 * pair + 1, :, columns] = odd.astype(jnp.bfloat16)


def pack(hidden, gain):
    tokens, features = hidden.shape
    return pl.pallas_call(
        pack_kernel,
        grid=(tokens // ROWS,),
        in_specs=[
            pl.BlockSpec((ROWS, features), lambda i: (i, 0)),
            pl.BlockSpec((1, features), lambda i: (0, 0)),
        ],
        out_specs=[
            pl.BlockSpec((PEERS, ROWS, features // PEERS), lambda i: (0, i, 0)),
            pl.BlockSpec((ROWS, 1), lambda i: (i, 0)),
        ],
        out_shape=[
            pltpu.HBM((PEERS, tokens, features // PEERS), jnp.bfloat16),
            jax.ShapeDtypeStruct((tokens, 1), jnp.float32),
        ],
        compiler_params=pltpu.CompilerParams(vmem_limit_bytes=KERNEL_VMEM),
        cost_estimate=pl.CostEstimate(
            flops=4 * tokens * features, bytes_accessed=4 * tokens * features, transcendentals=tokens
        ),
        name="pack_hidden",
    )(hidden, gain)


STEPS = 4
HELD = (0, -1, 1, 2)


def project_kernel(place_ref, tokens_ref, *refs):
    held_refs, (out_ref, weight) = refs[: len(HELD)], refs[len(HELD) :]

    @pl.when(pl.program_id(0) == 0)
    def _():
        for held_ref, above in zip(held_refs, HELD, strict=True):
            residue = lax.rem(place_ref[0] + above + STEPS, STEPS)
            for at in range(PLANES // STEPS):
                for nth in range(SIDES):
                    side = place_ref[1] if nth == 0 else 1 - place_ref[1]
                    start = (at * STEPS + residue) * 128 + side * 64
                    given = (at * SIDES + nth) * 64
                    weight[pl.ds(pl.multiple_of(start, 64), 64), :] = held_ref[given : given + 64, :]

    tokens = tokens_ref[...].reshape(-1, tokens_ref.shape[-1])
    product = jnp.dot(tokens, weight[...], preferred_element_type=jnp.float32)
    out_ref[...] = product.astype(jnp.bfloat16).reshape(out_ref.shape)


def project(place, tokens, held):
    sources, rows, features = tokens.shape
    width = held[0].shape[1]
    whole = [pl.BlockSpec(part.shape, lambda i, place: (0, 0)) for part in held]
    return pl.pallas_call(
        project_kernel,
        grid_spec=pltpu.PrefetchScalarGridSpec(
            num_scalar_prefetch=1,
            grid=(sources // SOURCES,),
            in_specs=[pl.BlockSpec((SOURCES, rows, features), lambda i, place: (i, 0, 0)), *whole],
            out_specs=pl.BlockSpec((SOURCES, rows, width), lambda i, place: (i, 0, 0)),
            scratch_shapes=[pltpu.VMEM((features, width), jnp.bfloat16)],
        ),
        out_shape=pltpu.HBM((sources, rows, width), jnp.bfloat16),
        compiler_params=pltpu.CompilerParams(vmem_limit_bytes=KERNEL_VMEM),
        cost_estimate=pl.CostEstimate(
            flops=2 * sources * rows * features * width,
            bytes_accessed=2 * (sources * rows * (features + width) + features * width),
            transcendentals=0,
        ),
        name="project_keys",
    )(place, tokens, *held)


def moved(block, target):
    return lax.ppermute(block, Z, [(z, target(z) % PLANES) for z in range(PLANES)])


def shards(
    hidden_in, norm_gain, key_weight, fragment_index, outer_params, outer_moment, inner_params
):
    replicas = 4
    layer_idx = fragment_index[0]
    outer_layer = lax.dynamic_index_in_dim(outer_params, layer_idx, 0, keepdims=False)
    inner_layer = lax.dynamic_index_in_dim(inner_params[0], layer_idx, 0, keepdims=False)
    pseudo_grad = (outer_layer - inner_layer.astype(jnp.float32)).astype(jnp.bfloat16)

    block = key_weight[0]
    block = jnp.concatenate([block, lax.ppermute(block, "yh", [(0, 1), (1, 0)])], axis=0)
    packed, scale = pack(hidden_in[0], norm_gain[None])
    packed, block, pseudo_grad = lax.optimization_barrier((packed, block, pseudo_grad))
    tokens = lax.all_to_all(packed, ROW, 0, 0, tiled=True)
    own = lax.all_gather(block, "zh", axis=0, tiled=True)
    own, pseudo_grad = lax.optimization_barrier((own, pseudo_grad))
    held = (
        own,
        moved(own, lambda z: z + 1),
        moved(own, lambda z: z - 1),
        moved(own, lambda z: z + 2 if z % 2 == 0 else z - 2),
    )
    others = []
    for other in range(1, replicas):
        pairs = [(replica, replica ^ other) for replica in range(replicas)]
        others.append(lax.ppermute(pseudo_grad, REP, pairs))
    place = jnp.stack([lax.axis_index(axis).astype(jnp.int32) for axis in ("zl", "yh")])
    partial = project(place, tokens, held)
    partial, layer_idx, others = lax.optimization_barrier((partial, layer_idx, others))
    partial = lax.all_to_all(partial, ROW, 0, 0, tiled=True)
    outer_layer = lax.dynamic_index_in_dim(outer_params, layer_idx, 0, keepdims=False)
    moment_layer = lax.dynamic_index_in_dim(outer_moment, layer_idx, 0, keepdims=False)
    inner_layer = lax.dynamic_index_in_dim(inner_params[0], layer_idx, 0, keepdims=False)
    summed = pseudo_grad.astype(jnp.float32) + sum(part.astype(jnp.float32) for part in others)
    new_outer, new_moment = outer_update(summed / replicas, outer_layer, moment_layer)
    mixed_inner = (
        mix_keep * inner_layer.astype(jnp.float32) + (1.0 - mix_keep) * new_outer
    ).astype(jnp.bfloat16)
    keys = (jnp.sum(partial.astype(jnp.float32), axis=0) * scale).astype(jnp.bfloat16)
    return (keys[None], new_outer, new_moment, mixed_inner[None])


def solution(mesh):
    fine = Mesh(mesh.devices.reshape(2, 2, 4, 4, 2, 4), ("yl", "core", "zh", "zl", "yh", "x"))
    fsdp = ("zh", "zl", "yh", "x")
    placed = (
        P(REP, fsdp, None),
        P(),
        P(REP, fsdp, None),
        P(),
        P(None, fsdp, None),
        P(None, fsdp, None),
        P(REP, None, fsdp, None),
    )
    return jax.shard_map(
        shards,
        mesh=fine,
        in_specs=placed,
        out_specs=(
            P(REP, fsdp, None),
            P(fsdp, None),
            P(fsdp, None),
            P(REP, fsdp, None),
        ),
        check_vma=False,
    )
```

```python
import jax
import jax.numpy as jnp
from jax import lax
from jax.experimental import pallas as pl
from jax.experimental.pallas import tpu as pltpu
from jax.sharding import Mesh, PartitionSpec as P

momentum_coef = 0.9
outer_rate = 0.7
mix_keep = 0.5
epsilon = 1e-05

Z, ROW, REP = ("zh", "zl"), "x", ("yl", "core")
PLANES, SIDES, PEERS = 16, 2, 4
ROWS, SOURCES = 64, 2
KERNEL_VMEM = 24 * 1024 * 1024


def outer_update(averaged, outer_layer, moment_layer):
    new_moment = momentum_coef * moment_layer + averaged
    new_outer = outer_layer - outer_rate * (averaged + momentum_coef * new_moment)
    return (new_outer, new_moment)


def pack_kernel(hidden_ref, gain_ref, packed_ref, scale_ref):
    hidden = hidden_ref[...].astype(jnp.float32)
    features = hidden.shape[1]
    mean_square = jnp.sum(hidden * hidden, axis=-1, keepdims=True) / features
    scale_ref[...] = lax.rsqrt(mean_square + epsilon)
    gained = hidden * gain_ref[...]
    low = lax.broadcasted_iota(jnp.int32, (hidden.shape[0], 128), 1) < 64
    for z in range(PLANES):
        for pair in range(PEERS // 2):
            start = z * 512 + pair * 128
            first, second = gained[:, start : start + 128], gained[:, start + 256 : start + 384]
            columns = slice(z * 128, z * 128 + 128)
            even = jnp.where(low, first, pltpu.roll(second, 64, 1))
            odd = jnp.where(low, pltpu.roll(first, 64, 1), second)
            packed_ref[2 * pair, :, columns] = even.astype(jnp.bfloat16)
            packed_ref[2 * pair + 1, :, columns] = odd.astype(jnp.bfloat16)


def pack(hidden, gain):
    tokens, features = hidden.shape
    return pl.pallas_call(
        pack_kernel,
        grid=(tokens // ROWS,),
        in_specs=[
            pl.BlockSpec((ROWS, features), lambda i: (i, 0)),
            pl.BlockSpec((1, features), lambda i: (0, 0)),
        ],
        out_specs=[
            pl.BlockSpec((PEERS, ROWS, features // PEERS), lambda i: (0, i, 0)),
            pl.BlockSpec((ROWS, 1), lambda i: (i, 0)),
        ],
        out_shape=[
            pltpu.HBM((PEERS, tokens, features // PEERS), jnp.bfloat16),
            jax.ShapeDtypeStruct((tokens, 1), jnp.float32),
        ],
        compiler_params=pltpu.CompilerParams(vmem_limit_bytes=KERNEL_VMEM),
        cost_estimate=pl.CostEstimate(
            flops=4 * tokens * features, bytes_accessed=4 * tokens * features, transcendentals=tokens
        ),
        name="pack_hidden",
    )(hidden, gain)


STEPS = 4
HELD = tuple((above, side) for side in range(SIDES) for above in (0, 2, -1, 1))


def project_kernel(place_ref, tokens_ref, *refs):
    held_refs, (out_ref, weight) = refs[: len(HELD)], refs[len(HELD) :]

    @pl.when(pl.program_id(0) == 0)
    def _():
        for held_ref, (above, other) in zip(held_refs, HELD, strict=True):
            residue = lax.rem(place_ref[0] + above + STEPS, STEPS)
            side = 1 - place_ref[1] if other else place_ref[1]
            for at in range(PLANES // STEPS):
                start = (at * STEPS + residue) * 128 + side * 64
                rows = pl.ds(pl.multiple_of(start, 64), 64)
                weight[rows, :] = held_ref[at * 64 : at * 64 + 64, :]

    tokens = tokens_ref[...].reshape(-1, tokens_ref.shape[-1])
    product = jnp.dot(tokens, weight[...], preferred_element_type=jnp.float32)
    out_ref[...] = product.astype(jnp.bfloat16).reshape(out_ref.shape)


def project(place, tokens, held):
    sources, rows, features = tokens.shape
    width = held[0].shape[1]
    whole = [pl.BlockSpec(part.shape, lambda i, place: (0, 0)) for part in held]
    return pl.pallas_call(
        project_kernel,
        grid_spec=pltpu.PrefetchScalarGridSpec(
            num_scalar_prefetch=1,
            grid=(sources // SOURCES,),
            in_specs=[pl.BlockSpec((SOURCES, rows, features), lambda i, place: (i, 0, 0)), *whole],
            out_specs=pl.BlockSpec((SOURCES, rows, width), lambda i, place: (i, 0, 0)),
            scratch_shapes=[pltpu.VMEM((features, width), jnp.bfloat16)],
        ),
        out_shape=pltpu.HBM((sources, rows, width), jnp.bfloat16),
        compiler_params=pltpu.CompilerParams(vmem_limit_bytes=KERNEL_VMEM),
        cost_estimate=pl.CostEstimate(
            flops=2 * sources * rows * features * width,
            bytes_accessed=2 * (sources * rows * (features + width) + features * width),
            transcendentals=0,
        ),
        name="project_keys",
    )(place, tokens, *held)


def moved(block, target):
    return lax.ppermute(block, Z, [(z, target(z) % PLANES) for z in range(PLANES)])


def shards(
    hidden_in, norm_gain, key_weight, fragment_index, outer_params, outer_moment, inner_params
):
    replicas = 4
    layer_idx = fragment_index[0]
    outer_layer = lax.dynamic_index_in_dim(outer_params, layer_idx, 0, keepdims=False)
    inner_layer = lax.dynamic_index_in_dim(inner_params[0], layer_idx, 0, keepdims=False)
    pseudo_grad = (outer_layer - inner_layer.astype(jnp.float32)).astype(jnp.bfloat16)

    packed, scale = pack(hidden_in[0], norm_gain[None])
    packed, block, pseudo_grad = lax.optimization_barrier((packed, key_weight[0], pseudo_grad))
    tokens = lax.all_to_all(packed, ROW, 0, 0, tiled=True)
    own = lax.all_gather(block, "zh", axis=0, tiled=True)
    held = [
        own,
        moved(own, lambda z: z + 2 if z % 2 == 0 else z - 2),
        moved(own, lambda z: z + 1),
        moved(own, lambda z: z - 1),
    ]
    held += [lax.ppermute(part, "yh", [(0, 1), (1, 0)]) for part in held]
    own, pseudo_grad = lax.optimization_barrier((held[3], pseudo_grad))
    others = []
    for other in range(1, replicas):
        pairs = [(replica, replica ^ other) for replica in range(replicas)]
        others.append(lax.ppermute(pseudo_grad, REP, pairs))
    place = jnp.stack([lax.axis_index(axis).astype(jnp.int32) for axis in ("zl", "yh")])
    partial = project(place, tokens, held)
    partial, layer_idx, others = lax.optimization_barrier((partial, layer_idx, others))
    partial = lax.all_to_all(partial, ROW, 0, 0, tiled=True)
    outer_layer = lax.dynamic_index_in_dim(outer_params, layer_idx, 0, keepdims=False)
    moment_layer = lax.dynamic_index_in_dim(outer_moment, layer_idx, 0, keepdims=False)
    inner_layer = lax.dynamic_index_in_dim(inner_params[0], layer_idx, 0, keepdims=False)
    summed = pseudo_grad.astype(jnp.float32) + sum(part.astype(jnp.float32) for part in others)
    new_outer, new_moment = outer_update(summed / replicas, outer_layer, moment_layer)
    mixed_inner = (
        mix_keep * inner_layer.astype(jnp.float32) + (1.0 - mix_keep) * new_outer
    ).astype(jnp.bfloat16)
    keys = (jnp.sum(partial.astype(jnp.float32), axis=0) * scale).astype(jnp.bfloat16)
    return (keys[None], new_outer, new_moment, mixed_inner[None])


def solution(mesh):
    fine = Mesh(mesh.devices.reshape(2, 2, 4, 4, 2, 4), ("yl", "core", "zh", "zl", "yh", "x"))
    fsdp = ("zh", "zl", "yh", "x")
    placed = (
        P(REP, fsdp, None),
        P(),
        P(REP, fsdp, None),
        P(),
        P(None, fsdp, None),
        P(None, fsdp, None),
        P(REP, None, fsdp, None),
    )
    return jax.shard_map(
        shards,
        mesh=fine,
        in_specs=placed,
        out_specs=(
            P(REP, fsdp, None),
            P(fsdp, None),
            P(fsdp, None),
            P(REP, fsdp, None),
        ),
        check_vma=False,
    )
```

```python
import jax
import jax.numpy as jnp
from jax import lax
from jax.experimental import pallas as pl
from jax.experimental.pallas import tpu as pltpu
from jax.sharding import Mesh, PartitionSpec as P

momentum_coef = 0.9
outer_rate = 0.7
mix_keep = 0.5
epsilon = 1e-05

Z, ROW, REP = ("zh", "zl"), "x", ("yl", "core")
PLANES, SIDES, PEERS = 16, 2, 4
ROWS, SOURCES = 64, 2
KERNEL_VMEM = 24 * 1024 * 1024


def outer_update(averaged, outer_layer, moment_layer):
    new_moment = momentum_coef * moment_layer + averaged
    new_outer = outer_layer - outer_rate * (averaged + momentum_coef * new_moment)
    return (new_outer, new_moment)


def pack_kernel(hidden_ref, gain_ref, packed_ref, scale_ref):
    hidden = hidden_ref[...].astype(jnp.float32)
    features = hidden.shape[1]
    mean_square = jnp.sum(hidden * hidden, axis=-1, keepdims=True) / features
    scale_ref[...] = lax.rsqrt(mean_square + epsilon)
    gained = hidden * gain_ref[...]
    low = lax.broadcasted_iota(jnp.int32, (hidden.shape[0], 128), 1) < 64
    for z in range(PLANES):
        for pair in range(PEERS // 2):
            start = z * 512 + pair * 128
            first, second = gained[:, start : start + 128], gained[:, start + 256 : start + 384]
            columns = slice(z * 128, z * 128 + 128)
            even = jnp.where(low, first, pltpu.roll(second, 64, 1))
            odd = jnp.where(low, pltpu.roll(first, 64, 1), second)
            packed_ref[2 * pair, :, columns] = even.astype(jnp.bfloat16)
            packed_ref[2 * pair + 1, :, columns] = odd.astype(jnp.bfloat16)


def pack(hidden, gain):
    tokens, features = hidden.shape
    return pl.pallas_call(
        pack_kernel,
        grid=(tokens // ROWS,),
        in_specs=[
            pl.BlockSpec((ROWS, features), lambda i: (i, 0)),
            pl.BlockSpec((1, features), lambda i: (0, 0)),
        ],
        out_specs=[
            pl.BlockSpec((PEERS, ROWS, features // PEERS), lambda i: (0, i, 0)),
            pl.BlockSpec((ROWS, 1), lambda i: (i, 0)),
        ],
        out_shape=[
            pltpu.HBM((PEERS, tokens, features // PEERS), jnp.bfloat16),
            jax.ShapeDtypeStruct((tokens, 1), jnp.float32),
        ],
        compiler_params=pltpu.CompilerParams(vmem_limit_bytes=KERNEL_VMEM),
        cost_estimate=pl.CostEstimate(
            flops=4 * tokens * features, bytes_accessed=4 * tokens * features, transcendentals=tokens
        ),
        name="pack_hidden",
    )(hidden, gain)


STEPS = 4
HELD = tuple((above, side) for side in range(SIDES) for above in (0, 2, -1, 1))


def project_kernel(place_ref, tokens_ref, *refs):
    held_refs, (out_ref, weight) = refs[: len(HELD)], refs[len(HELD) :]

    @pl.when(pl.program_id(0) == 0)
    def _():
        for held_ref, (above, other) in zip(held_refs, HELD, strict=True):
            residue = lax.rem(place_ref[0] + above + STEPS, STEPS)
            side = 1 - place_ref[1] if other else place_ref[1]
            for at in range(PLANES // STEPS):
                start = (at * STEPS + residue) * 128 + side * 64
                rows = pl.ds(pl.multiple_of(start, 64), 64)
                weight[rows, :] = held_ref[at * 64 : at * 64 + 64, :]

    tokens = tokens_ref[...].reshape(-1, tokens_ref.shape[-1])
    product = jnp.dot(tokens, weight[...], preferred_element_type=jnp.float32)
    out_ref[...] = product.astype(jnp.bfloat16).reshape(out_ref.shape)


def project(place, tokens, held):
    sources, rows, features = tokens.shape
    width = held[0].shape[1]
    whole = [pl.BlockSpec(part.shape, lambda i, place: (0, 0)) for part in held]
    return pl.pallas_call(
        project_kernel,
        grid_spec=pltpu.PrefetchScalarGridSpec(
            num_scalar_prefetch=1,
            grid=(sources // SOURCES,),
            in_specs=[pl.BlockSpec((SOURCES, rows, features), lambda i, place: (i, 0, 0)), *whole],
            out_specs=pl.BlockSpec((SOURCES, rows, width), lambda i, place: (i, 0, 0)),
            scratch_shapes=[pltpu.VMEM((features, width), jnp.bfloat16)],
        ),
        out_shape=pltpu.HBM((sources, rows, width), jnp.bfloat16),
        compiler_params=pltpu.CompilerParams(vmem_limit_bytes=KERNEL_VMEM),
        cost_estimate=pl.CostEstimate(
            flops=2 * sources * rows * features * width,
            bytes_accessed=2 * (sources * rows * (features + width) + features * width),
            transcendentals=0,
        ),
        name="project_keys",
    )(place, tokens, *held)


def moved(block, target):
    return lax.ppermute(block, Z, [(z, target(z) % PLANES) for z in range(PLANES)])


def shards(
    hidden_in, norm_gain, key_weight, fragment_index, outer_params, outer_moment, inner_params
):
    replicas = 4
    packed, scale = pack(hidden_in[0], norm_gain[None])
    packed, block = lax.optimization_barrier((packed, key_weight[0]))
    tokens = lax.all_to_all(packed, ROW, 0, 0, tiled=True)
    own = lax.all_gather(block, "zh", axis=0, tiled=True)
    held = [
        own,
        moved(own, lambda z: z + 2 if z % 2 == 0 else z - 2),
        moved(own, lambda z: z + 1),
        moved(own, lambda z: z - 1),
    ]
    held += [lax.ppermute(part, "yh", [(0, 1), (1, 0)]) for part in held]
    held[1], fragment_index = lax.optimization_barrier((held[1], fragment_index))
    layer_idx = fragment_index[0]
    outer_layer = lax.dynamic_index_in_dim(outer_params, layer_idx, 0, keepdims=False)
    inner_layer = lax.dynamic_index_in_dim(inner_params[0], layer_idx, 0, keepdims=False)
    pseudo_grad = (outer_layer - inner_layer.astype(jnp.float32)).astype(jnp.bfloat16)
    place = jnp.stack([lax.axis_index(axis).astype(jnp.int32) for axis in ("zl", "yh")])
    partial = project(place, tokens, held)
    partial, layer_idx, pseudo_grad = lax.optimization_barrier((partial, layer_idx, pseudo_grad))
    partial = lax.all_to_all(partial, ROW, 0, 0, tiled=True)
    others = []
    for other in range(1, replicas):
        pairs = [(replica, replica ^ other) for replica in range(replicas)]
        others.append(lax.ppermute(pseudo_grad, REP, pairs))
    outer_layer = lax.dynamic_index_in_dim(outer_params, layer_idx, 0, keepdims=False)
    moment_layer = lax.dynamic_index_in_dim(outer_moment, layer_idx, 0, keepdims=False)
    inner_layer = lax.dynamic_index_in_dim(inner_params[0], layer_idx, 0, keepdims=False)
    summed = pseudo_grad.astype(jnp.float32) + sum(part.astype(jnp.float32) for part in others)
    new_outer, new_moment = outer_update(summed / replicas, outer_layer, moment_layer)
    mixed_inner = (
        mix_keep * inner_layer.astype(jnp.float32) + (1.0 - mix_keep) * new_outer
    ).astype(jnp.bfloat16)
    keys = (jnp.sum(partial.astype(jnp.float32), axis=0) * scale).astype(jnp.bfloat16)
    return (keys[None], new_outer, new_moment, mixed_inner[None])


def solution(mesh):
    fine = Mesh(mesh.devices.reshape(2, 2, 4, 4, 2, 4), ("yl", "core", "zh", "zl", "yh", "x"))
    fsdp = ("zh", "zl", "yh", "x")
    placed = (
        P(REP, fsdp, None),
        P(),
        P(REP, fsdp, None),
        P(),
        P(None, fsdp, None),
        P(None, fsdp, None),
        P(REP, None, fsdp, None),
    )
    return jax.shard_map(
        shards,
        mesh=fine,
        in_specs=placed,
        out_specs=(
            P(REP, fsdp, None),
            P(fsdp, None),
            P(fsdp, None),
            P(REP, fsdp, None),
        ),
        check_vma=False,
    )
```

```python
import jax
import jax.numpy as jnp
from jax import lax
from jax.experimental import pallas as pl
from jax.experimental.pallas import tpu as pltpu
from jax.sharding import Mesh, PartitionSpec as P

momentum_coef = 0.9
outer_rate = 0.7
mix_keep = 0.5
epsilon = 1e-05

Z, PLANE, REP = ("zh", "zl"), ("yh", "x"), ("yl", "core")
PLANES, PEERS = 16, 8
ROWS, SOURCES = 64, 4
KERNEL_VMEM = 24 * 1024 * 1024


def outer_update(averaged, outer_layer, moment_layer):
    new_moment = momentum_coef * moment_layer + averaged
    new_outer = outer_layer - outer_rate * (averaged + momentum_coef * new_moment)
    return (new_outer, new_moment)


def pack_kernel(hidden_ref, gain_ref, packed_ref, scale_ref):
    hidden = hidden_ref[...].astype(jnp.float32)
    features = hidden.shape[1]
    mean_square = jnp.sum(hidden * hidden, axis=-1, keepdims=True) / features
    scale_ref[...] = lax.rsqrt(mean_square + epsilon)
    gained = hidden * gain_ref[...]
    low = lax.broadcasted_iota(jnp.int32, (hidden.shape[0], 128), 1) < 64
    for pair in range(PLANES // 2):
        for tile in range(PEERS // 2):
            start = pair * 1024 + tile * 128
            first = gained[:, start : start + 128]
            second = gained[:, start + 512 : start + 640]
            columns = slice(pair * 128, pair * 128 + 128)
            even = jnp.where(low, first, pltpu.roll(second, 64, 1))
            odd = jnp.where(low, pltpu.roll(first, 64, 1), second)
            packed_ref[2 * tile, :, columns] = even.astype(jnp.bfloat16)
            packed_ref[2 * tile + 1, :, columns] = odd.astype(jnp.bfloat16)


def pack(hidden, gain):
    tokens, features = hidden.shape
    return pl.pallas_call(
        pack_kernel,
        grid=(tokens // ROWS,),
        in_specs=[
            pl.BlockSpec((ROWS, features), lambda i: (i, 0)),
            pl.BlockSpec((1, features), lambda i: (0, 0)),
        ],
        out_specs=[
            pl.BlockSpec((PEERS, ROWS, features // PEERS), lambda i: (0, i, 0)),
            pl.BlockSpec((ROWS, 1), lambda i: (i, 0)),
        ],
        out_shape=[
            pltpu.HBM((PEERS, tokens, features // PEERS), jnp.bfloat16),
            jax.ShapeDtypeStruct((tokens, 1), jnp.float32),
        ],
        compiler_params=pltpu.CompilerParams(vmem_limit_bytes=KERNEL_VMEM),
        cost_estimate=pl.CostEstimate(
            flops=4 * tokens * features, bytes_accessed=4 * tokens * features, transcendentals=tokens
        ),
        name="pack_hidden",
    )(hidden, gain)


STEPS = 4
HELD = (0, 2, -1, 1)


def project_kernel(residue_ref, tokens_ref, *refs):
    held_refs, (out_ref, weight) = refs[: len(HELD)], refs[len(HELD) :]

    @pl.when(pl.program_id(0) == 0)
    def _():
        for held_ref, above in zip(held_refs, HELD, strict=True):
            residue = lax.rem(residue_ref[0] + above + STEPS, STEPS)
            for at in range(PLANES // STEPS):
                rows = pl.ds(pl.multiple_of((at * STEPS + residue) * 64, 64), 64)
                weight[rows, :] = held_ref[at * 64 : at * 64 + 64, :]

    tokens = tokens_ref[...].reshape(-1, tokens_ref.shape[-1])
    product = jnp.dot(tokens, weight[...], preferred_element_type=jnp.float32)
    out_ref[...] = product.astype(jnp.bfloat16).reshape(out_ref.shape)


def project(residue, tokens, held):
    peers, rows, features = tokens.shape
    width = held[0].shape[1]
    whole = [pl.BlockSpec(part.shape, lambda i, residue: (0, 0)) for part in held]
    return pl.pallas_call(
        project_kernel,
        grid_spec=pltpu.PrefetchScalarGridSpec(
            num_scalar_prefetch=1,
            grid=(peers // SOURCES,),
            in_specs=[pl.BlockSpec((SOURCES, rows, features), lambda i, residue: (i, 0, 0)), *whole],
            out_specs=pl.BlockSpec((SOURCES, rows, width), lambda i, residue: (i, 0, 0)),
            scratch_shapes=[pltpu.VMEM((features, width), jnp.bfloat16)],
        ),
        out_shape=pltpu.HBM((peers, rows, width), jnp.bfloat16),
        compiler_params=pltpu.CompilerParams(vmem_limit_bytes=KERNEL_VMEM),
        cost_estimate=pl.CostEstimate(
            flops=2 * peers * rows * features * width,
            bytes_accessed=2 * (peers * rows * (features + width) + features * width),
            transcendentals=0,
        ),
        name="project_keys",
    )(residue, tokens, *held)


def moved(block, target):
    return lax.ppermute(block, Z, [(z, target(z) % PLANES) for z in range(PLANES)])


def shards(
    hidden_in, norm_gain, key_weight, fragment_index, outer_params, outer_moment, inner_params
):
    replicas = 4
    packed, scale = pack(hidden_in[0], norm_gain[None])
    packed, block = lax.optimization_barrier((packed, key_weight[0]))
    tokens = lax.all_to_all(packed, PLANE, 0, 0, tiled=True)
    own = lax.all_gather(block, "zh", axis=0, tiled=True)
    held = (
        own,
        moved(own, lambda z: z + 2 if z % 2 == 0 else z - 2),
        moved(own, lambda z: z + 1),
        moved(own, lambda z: z - 1),
    )
    _, fragment_index = lax.optimization_barrier((own, fragment_index))
    layer_idx = fragment_index[0]
    outer_layer = lax.dynamic_index_in_dim(outer_params, layer_idx, 0, keepdims=False)
    inner_layer = lax.dynamic_index_in_dim(inner_params[0], layer_idx, 0, keepdims=False)
    pseudo_grad = (outer_layer - inner_layer.astype(jnp.float32)).astype(jnp.bfloat16)
    others = []
    for other in range(1, replicas):
        pairs = [(replica, replica ^ other) for replica in range(replicas)]
        others.append(lax.ppermute(pseudo_grad, REP, pairs))
    residue = lax.axis_index("zl").astype(jnp.int32)[None]
    partial = project(residue, tokens, held)
    partial, layer_idx, others = lax.optimization_barrier((partial, layer_idx, others))
    partial = lax.all_to_all(partial, PLANE, 0, 0, tiled=True)
    outer_layer = lax.dynamic_index_in_dim(outer_params, layer_idx, 0, keepdims=False)
    moment_layer = lax.dynamic_index_in_dim(outer_moment, layer_idx, 0, keepdims=False)
    inner_layer = lax.dynamic_index_in_dim(inner_params[0], layer_idx, 0, keepdims=False)
    summed = pseudo_grad.astype(jnp.float32) + sum(part.astype(jnp.float32) for part in others)
    new_outer, new_moment = outer_update(summed / replicas, outer_layer, moment_layer)
    mixed_inner = (
        mix_keep * inner_layer.astype(jnp.float32) + (1.0 - mix_keep) * new_outer
    ).astype(jnp.bfloat16)
    keys = (jnp.sum(partial.astype(jnp.float32), axis=0) * scale).astype(jnp.bfloat16)
    return (keys[None], new_outer, new_moment, mixed_inner[None])


def solution(mesh):
    fine = Mesh(mesh.devices.reshape(2, 2, 4, 4, 2, 4), ("yl", "core", "zh", "zl", "yh", "x"))
    fsdp = ("zh", "zl", "yh", "x")
    placed = (
        P(REP, fsdp, None),
        P(),
        P(REP, fsdp, None),
        P(),
        P(None, fsdp, None),
        P(None, fsdp, None),
        P(REP, None, fsdp, None),
    )
    return jax.shard_map(
        shards,
        mesh=fine,
        in_specs=placed,
        out_specs=(
            P(REP, fsdp, None),
            P(fsdp, None),
            P(fsdp, None),
            P(REP, fsdp, None),
        ),
        check_vma=False,
    )
```

```python
import jax
import jax.numpy as jnp
from jax import lax
from jax.experimental import pallas as pl
from jax.experimental.pallas import tpu as pltpu
from jax.sharding import Mesh, PartitionSpec as P

momentum_coef = 0.9
outer_rate = 0.7
mix_keep = 0.5
epsilon = 1e-05

Z, PLANE, REP = ("zh", "zl"), ("yh", "x"), ("yl", "core")
PLANES, PEERS = 16, 8
ROWS, SOURCES = 96, 4
PACK_VMEM, PROJECT_VMEM = 60 * 1024 * 1024, 24 * 1024 * 1024


def outer_update(averaged, outer_layer, moment_layer):
    new_moment = momentum_coef * moment_layer + averaged
    new_outer = outer_layer - outer_rate * (averaged + momentum_coef * new_moment)
    return (new_outer, new_moment)


def pack_kernel(hidden_ref, gain_ref, packed_ref, scale_ref):
    hidden = hidden_ref[...].astype(jnp.float32)
    features = hidden.shape[1]
    mean_square = jnp.sum(hidden * hidden, axis=-1, keepdims=True) / features
    scale_ref[...] = lax.rsqrt(mean_square + epsilon)
    gained = hidden * gain_ref[...]
    low = lax.broadcasted_iota(jnp.int32, (hidden.shape[0], 128), 1) < 64
    for pair in range(PLANES // 2):
        for tile in range(PEERS // 2):
            start = pair * 1024 + tile * 128
            first = gained[:, start : start + 128]
            second = gained[:, start + 512 : start + 640]
            columns = slice(pair * 128, pair * 128 + 128)
            even = jnp.where(low, first, pltpu.roll(second, 64, 1))
            odd = jnp.where(low, pltpu.roll(first, 64, 1), second)
            packed_ref[2 * tile, :, columns] = even.astype(jnp.bfloat16)
            packed_ref[2 * tile + 1, :, columns] = odd.astype(jnp.bfloat16)


def pack(hidden, gain):
    tokens, features = hidden.shape
    return pl.pallas_call(
        pack_kernel,
        grid=(tokens // ROWS,),
        in_specs=[
            pl.BlockSpec((ROWS, features), lambda i: (i, 0)),
            pl.BlockSpec((1, features), lambda i: (0, 0)),
        ],
        out_specs=[
            pl.BlockSpec((PEERS, ROWS, features // PEERS), lambda i: (0, i, 0)),
            pl.BlockSpec((ROWS, 1), lambda i: (i, 0)),
        ],
        out_shape=[
            pltpu.HBM((PEERS, tokens, features // PEERS), jnp.bfloat16),
            jax.ShapeDtypeStruct((tokens, 1), jnp.float32),
        ],
        compiler_params=pltpu.CompilerParams(vmem_limit_bytes=PACK_VMEM),
        cost_estimate=pl.CostEstimate(
            flops=4 * tokens * features, bytes_accessed=4 * tokens * features, transcendentals=tokens
        ),
        name="pack_hidden",
    )(hidden, gain)


STEPS = 4
HELD = (0, 2, -1, 1)


def project_kernel(residue_ref, tokens_ref, *refs):
    held_refs, (out_ref, weight) = refs[: len(HELD)], refs[len(HELD) :]

    @pl.when(pl.program_id(0) == 0)
    def _():
        for held_ref, above in zip(held_refs, HELD, strict=True):
            residue = lax.rem(residue_ref[0] + above + STEPS, STEPS)
            for at in range(PLANES // STEPS):
                rows = pl.ds(pl.multiple_of((at * STEPS + residue) * 64, 64), 64)
                weight[rows, :] = held_ref[at * 64 : at * 64 + 64, :]

    tokens = tokens_ref[...].reshape(-1, tokens_ref.shape[-1])
    product = jnp.dot(tokens, weight[...], preferred_element_type=jnp.float32)
    out_ref[...] = product.astype(jnp.bfloat16).reshape(out_ref.shape)


def project(residue, tokens, held):
    peers, rows, features = tokens.shape
    width = held[0].shape[1]
    whole = [pl.BlockSpec(part.shape, lambda i, residue: (0, 0)) for part in held]
    return pl.pallas_call(
        project_kernel,
        grid_spec=pltpu.PrefetchScalarGridSpec(
            num_scalar_prefetch=1,
            grid=(peers // SOURCES,),
            in_specs=[pl.BlockSpec((SOURCES, rows, features), lambda i, residue: (i, 0, 0)), *whole],
            out_specs=pl.BlockSpec((SOURCES, rows, width), lambda i, residue: (i, 0, 0)),
            scratch_shapes=[pltpu.VMEM((features, width), jnp.bfloat16)],
        ),
        out_shape=pltpu.HBM((peers, rows, width), jnp.bfloat16),
        compiler_params=pltpu.CompilerParams(vmem_limit_bytes=PROJECT_VMEM),
        cost_estimate=pl.CostEstimate(
            flops=2 * peers * rows * features * width,
            bytes_accessed=2 * (peers * rows * (features + width) + features * width),
            transcendentals=0,
        ),
        name="project_keys",
    )(residue, tokens, *held)


def moved(block, target):
    return lax.ppermute(block, Z, [(z, target(z) % PLANES) for z in range(PLANES)])


def shards(
    hidden_in, norm_gain, key_weight, fragment_index, outer_params, outer_moment, inner_params
):
    replicas = 4
    packed, scale = pack(hidden_in[0], norm_gain[None])
    packed, block = lax.optimization_barrier((packed, key_weight[0]))
    tokens = lax.all_to_all(packed, PLANE, 0, 0, tiled=True)
    own = lax.all_gather(block, "zh", axis=0, tiled=True)
    held = (
        own,
        moved(own, lambda z: z + 2 if z % 2 == 0 else z - 2),
        moved(own, lambda z: z + 1),
        moved(own, lambda z: z - 1),
    )
    residue = lax.axis_index("zl").astype(jnp.int32)[None]
    partial = project(residue, tokens, held)
    partial, fragment_index = lax.optimization_barrier((partial, fragment_index))
    partial = lax.all_to_all(partial, PLANE, 0, 0, tiled=True)
    layer_idx = fragment_index[0]
    outer_layer = lax.dynamic_index_in_dim(outer_params, layer_idx, 0, keepdims=False)
    moment_layer = lax.dynamic_index_in_dim(outer_moment, layer_idx, 0, keepdims=False)
    inner_layer = lax.dynamic_index_in_dim(inner_params[0], layer_idx, 0, keepdims=False)
    pseudo_grad = (outer_layer - inner_layer.astype(jnp.float32)).astype(jnp.bfloat16)
    summed = pseudo_grad.astype(jnp.float32)
    for other in range(1, replicas):
        pairs = [(replica, replica ^ other) for replica in range(replicas)]
        summed += lax.ppermute(pseudo_grad, REP, pairs).astype(jnp.float32)
    new_outer, new_moment = outer_update(summed / replicas, outer_layer, moment_layer)
    mixed_inner = (
        mix_keep * inner_layer.astype(jnp.float32) + (1.0 - mix_keep) * new_outer
    ).astype(jnp.bfloat16)
    keys = (jnp.sum(partial.astype(jnp.float32), axis=0) * scale).astype(jnp.bfloat16)
    return (keys[None], new_outer, new_moment, mixed_inner[None])


def solution(mesh):
    fine = Mesh(mesh.devices.reshape(2, 2, 4, 4, 2, 4), ("yl", "core", "zh", "zl", "yh", "x"))
    fsdp = ("zh", "zl", "yh", "x")
    placed = (
        P(REP, fsdp, None),
        P(),
        P(REP, fsdp, None),
        P(),
        P(None, fsdp, None),
        P(None, fsdp, None),
        P(REP, None, fsdp, None),
    )
    return jax.shard_map(
        shards,
        mesh=fine,
        in_specs=placed,
        out_specs=(
            P(REP, fsdp, None),
            P(fsdp, None),
            P(fsdp, None),
            P(REP, fsdp, None),
        ),
        check_vma=False,
    )
```

```python
import jax
import jax.numpy as jnp
from jax import lax
from jax.experimental import pallas as pl
from jax.experimental.pallas import tpu as pltpu
from jax.sharding import Mesh, PartitionSpec as P

momentum_coef = 0.9
outer_rate = 0.7
mix_keep = 0.5
epsilon = 1e-05

Z, PLANE, REP = ("zh", "zl"), ("yh", "x"), ("yl", "core")
PLANES, PEERS = 16, 8
ROWS, SOURCES = 96, 4
PACK_VMEM, PROJECT_VMEM = 60 * 1024 * 1024, 24 * 1024 * 1024


def outer_update(averaged, outer_layer, moment_layer):
    new_moment = momentum_coef * moment_layer + averaged
    new_outer = outer_layer - outer_rate * (averaged + momentum_coef * new_moment)
    return (new_outer, new_moment)


def pack_kernel(hidden_ref, gain_ref, packed_ref, scale_ref):
    hidden = hidden_ref[...].astype(jnp.float32)
    features = hidden.shape[1]
    mean_square = jnp.sum(hidden * hidden, axis=-1, keepdims=True) / features
    scale_ref[...] = lax.rsqrt(mean_square + epsilon)
    gained = hidden * gain_ref[...]
    low = lax.broadcasted_iota(jnp.int32, (hidden.shape[0], 128), 1) < 64
    for pair in range(PLANES // 2):
        for tile in range(PEERS // 2):
            start = pair * 1024 + tile * 128
            first = gained[:, start : start + 128]
            second = gained[:, start + 512 : start + 640]
            columns = slice(pair * 128, pair * 128 + 128)
            even = jnp.where(low, first, pltpu.roll(second, 64, 1))
            odd = jnp.where(low, pltpu.roll(first, 64, 1), second)
            packed_ref[2 * tile, :, columns] = even.astype(jnp.bfloat16)
            packed_ref[2 * tile + 1, :, columns] = odd.astype(jnp.bfloat16)


def pack(hidden, gain):
    tokens, features = hidden.shape
    return pl.pallas_call(
        pack_kernel,
        grid=(tokens // ROWS,),
        in_specs=[
            pl.BlockSpec((ROWS, features), lambda i: (i, 0)),
            pl.BlockSpec((1, features), lambda i: (0, 0)),
        ],
        out_specs=[
            pl.BlockSpec((PEERS, ROWS, features // PEERS), lambda i: (0, i, 0)),
            pl.BlockSpec((ROWS, 1), lambda i: (i, 0)),
        ],
        out_shape=[
            pltpu.HBM((PEERS, tokens, features // PEERS), jnp.bfloat16),
            jax.ShapeDtypeStruct((tokens, 1), jnp.float32),
        ],
        compiler_params=pltpu.CompilerParams(vmem_limit_bytes=PACK_VMEM),
        cost_estimate=pl.CostEstimate(
            flops=4 * tokens * features, bytes_accessed=4 * tokens * features, transcendentals=tokens
        ),
        name="pack_hidden",
    )(hidden, gain)


STEPS = 4
HELD = (0, 1, -1, 2)


def project_kernel(residue_ref, tokens_ref, *refs):
    held_refs, (out_ref, weight) = refs[: len(HELD)], refs[len(HELD) :]

    @pl.when(pl.program_id(0) == 0)
    def _():
        for held_ref, above in zip(held_refs, HELD, strict=True):
            residue = lax.rem(residue_ref[0] + above + STEPS, STEPS)
            for at in range(PLANES // STEPS):
                rows = pl.ds(pl.multiple_of((at * STEPS + residue) * 64, 64), 64)
                weight[rows, :] = held_ref[at * 64 : at * 64 + 64, :]

    tokens = tokens_ref[...].reshape(-1, tokens_ref.shape[-1])
    product = jnp.dot(tokens, weight[...], preferred_element_type=jnp.float32)
    out_ref[...] = product.astype(jnp.bfloat16).reshape(out_ref.shape)


def project(residue, tokens, held):
    peers, rows, features = tokens.shape
    width = held[0].shape[1]
    whole = [pl.BlockSpec(part.shape, lambda i, residue: (0, 0)) for part in held]
    return pl.pallas_call(
        project_kernel,
        grid_spec=pltpu.PrefetchScalarGridSpec(
            num_scalar_prefetch=1,
            grid=(peers // SOURCES,),
            in_specs=[pl.BlockSpec((SOURCES, rows, features), lambda i, residue: (i, 0, 0)), *whole],
            out_specs=pl.BlockSpec((SOURCES, rows, width), lambda i, residue: (i, 0, 0)),
            scratch_shapes=[pltpu.VMEM((features, width), jnp.bfloat16)],
        ),
        out_shape=pltpu.HBM((peers, rows, width), jnp.bfloat16),
        compiler_params=pltpu.CompilerParams(vmem_limit_bytes=PROJECT_VMEM),
        cost_estimate=pl.CostEstimate(
            flops=2 * peers * rows * features * width,
            bytes_accessed=2 * (peers * rows * (features + width) + features * width),
            transcendentals=0,
        ),
        name="project_keys",
    )(residue, tokens, *held)


def moved(block, target):
    return lax.ppermute(block, Z, [(z, target(z) % PLANES) for z in range(PLANES)])


def shards(
    hidden_in, norm_gain, key_weight, fragment_index, outer_params, outer_moment, inner_params
):
    replicas = 4
    packed, scale = pack(hidden_in[0], norm_gain[None])
    packed, block = lax.optimization_barrier((packed, key_weight[0]))
    tokens = lax.all_to_all(packed, PLANE, 0, 0, tiled=True)
    own = lax.all_gather(block, "zh", axis=0, tiled=True)
    held = (
        own,
        moved(own, lambda z: z - 1),
        moved(own, lambda z: z + 1),
        moved(own, lambda z: z + 2 if z % 2 == 0 else z - 2),
    )
    _, fragment_index = lax.optimization_barrier((own, fragment_index))
    layer_idx = fragment_index[0]
    outer_layer = lax.dynamic_index_in_dim(outer_params, layer_idx, 0, keepdims=False)
    inner_layer = lax.dynamic_index_in_dim(inner_params[0], layer_idx, 0, keepdims=False)
    pseudo_grad = (outer_layer - inner_layer.astype(jnp.float32)).astype(jnp.bfloat16)
    residue = lax.axis_index("zl").astype(jnp.int32)[None]
    partial = project(residue, tokens, held)
    partial, layer_idx, pseudo_grad = lax.optimization_barrier((partial, layer_idx, pseudo_grad))
    partial = lax.all_to_all(partial, PLANE, 0, 0, tiled=True)
    outer_layer = lax.dynamic_index_in_dim(outer_params, layer_idx, 0, keepdims=False)
    moment_layer = lax.dynamic_index_in_dim(outer_moment, layer_idx, 0, keepdims=False)
    inner_layer = lax.dynamic_index_in_dim(inner_params[0], layer_idx, 0, keepdims=False)
    summed = pseudo_grad.astype(jnp.float32)
    for other in range(1, replicas):
        pairs = [(replica, replica ^ other) for replica in range(replicas)]
        summed += lax.ppermute(pseudo_grad, REP, pairs).astype(jnp.float32)
    new_outer, new_moment = outer_update(summed / replicas, outer_layer, moment_layer)
    mixed_inner = (
        mix_keep * inner_layer.astype(jnp.float32) + (1.0 - mix_keep) * new_outer
    ).astype(jnp.bfloat16)
    keys = (jnp.sum(partial.astype(jnp.float32), axis=0) * scale).astype(jnp.bfloat16)
    return (keys[None], new_outer, new_moment, mixed_inner[None])


def solution(mesh):
    fine = Mesh(mesh.devices.reshape(2, 2, 4, 4, 2, 4), ("yl", "core", "zh", "zl", "yh", "x"))
    fsdp = ("zh", "zl", "yh", "x")
    placed = (
        P(REP, fsdp, None),
        P(),
        P(REP, fsdp, None),
        P(),
        P(None, fsdp, None),
        P(None, fsdp, None),
        P(REP, None, fsdp, None),
    )
    return jax.shard_map(
        shards,
        mesh=fine,
        in_specs=placed,
        out_specs=(
            P(REP, fsdp, None),
            P(fsdp, None),
            P(fsdp, None),
            P(REP, fsdp, None),
        ),
        check_vma=False,
    )
```

```python
import jax
import jax.numpy as jnp
from jax import lax
from jax.experimental import pallas as pl
from jax.experimental.pallas import tpu as pltpu
from jax.sharding import Mesh, PartitionSpec as P

momentum_coef = 0.9
outer_rate = 0.7
mix_keep = 0.5
epsilon = 1e-05

Z, PLANE, REP = ("zh", "zl"), ("yh", "x"), ("yl", "core")
PLANES, PEERS = 16, 8
ROWS, SOURCES = 96, 4
PACK_VMEM, PROJECT_VMEM = 60 * 1024 * 1024, 24 * 1024 * 1024


def outer_update(averaged, outer_layer, moment_layer):
    new_moment = momentum_coef * moment_layer + averaged
    new_outer = outer_layer - outer_rate * (averaged + momentum_coef * new_moment)
    return (new_outer, new_moment)


def pack_kernel(hidden_ref, gain_ref, packed_ref, scale_ref):
    hidden = hidden_ref[...].astype(jnp.float32)
    features = hidden.shape[1]
    mean_square = jnp.sum(hidden * hidden, axis=-1, keepdims=True) / features
    scale_ref[...] = lax.rsqrt(mean_square + epsilon)
    gained = hidden * gain_ref[...]
    low = lax.broadcasted_iota(jnp.int32, (hidden.shape[0], 128), 1) < 64
    for pair in range(PLANES // 2):
        for tile in range(PEERS // 2):
            start = pair * 1024 + tile * 128
            first = gained[:, start : start + 128]
            second = gained[:, start + 512 : start + 640]
            columns = slice(pair * 128, pair * 128 + 128)
            even = jnp.where(low, first, pltpu.roll(second, 64, 1))
            odd = jnp.where(low, pltpu.roll(first, 64, 1), second)
            packed_ref[2 * tile, :, columns] = even.astype(jnp.bfloat16)
            packed_ref[2 * tile + 1, :, columns] = odd.astype(jnp.bfloat16)


def pack(hidden, gain):
    tokens, features = hidden.shape
    return pl.pallas_call(
        pack_kernel,
        grid=(tokens // ROWS,),
        in_specs=[
            pl.BlockSpec((ROWS, features), lambda i: (i, 0)),
            pl.BlockSpec((1, features), lambda i: (0, 0)),
        ],
        out_specs=[
            pl.BlockSpec((PEERS, ROWS, features // PEERS), lambda i: (0, i, 0)),
            pl.BlockSpec((ROWS, 1), lambda i: (i, 0)),
        ],
        out_shape=[
            pltpu.HBM((PEERS, tokens, features // PEERS), jnp.bfloat16),
            jax.ShapeDtypeStruct((tokens, 1), jnp.float32),
        ],
        compiler_params=pltpu.CompilerParams(vmem_limit_bytes=PACK_VMEM),
        cost_estimate=pl.CostEstimate(
            flops=4 * tokens * features, bytes_accessed=4 * tokens * features, transcendentals=tokens
        ),
        name="pack_hidden",
    )(hidden, gain)


STEPS = 4
HELD = (0, 1, -1, 2)


def project_kernel(residue_ref, tokens_ref, *refs):
    held_refs, (out_ref, weight) = refs[: len(HELD)], refs[len(HELD) :]

    @pl.when(pl.program_id(0) == 0)
    def _():
        for held_ref, above in zip(held_refs, HELD, strict=True):
            residue = lax.rem(residue_ref[0] + above + STEPS, STEPS)
            for at in range(PLANES // STEPS):
                rows = pl.ds(pl.multiple_of((at * STEPS + residue) * 64, 64), 64)
                weight[rows, :] = held_ref[at * 64 : at * 64 + 64, :]

    tokens = tokens_ref[...].reshape(-1, tokens_ref.shape[-1])
    product = jnp.dot(tokens, weight[...], preferred_element_type=jnp.float32)
    out_ref[...] = product.astype(jnp.bfloat16).reshape(out_ref.shape)


def project(residue, tokens, held):
    peers, rows, features = tokens.shape
    width = held[0].shape[1]
    whole = [pl.BlockSpec(part.shape, lambda i, residue: (0, 0)) for part in held]
    return pl.pallas_call(
        project_kernel,
        grid_spec=pltpu.PrefetchScalarGridSpec(
            num_scalar_prefetch=1,
            grid=(peers // SOURCES,),
            in_specs=[pl.BlockSpec((SOURCES, rows, features), lambda i, residue: (i, 0, 0)), *whole],
            out_specs=pl.BlockSpec((SOURCES, rows, width), lambda i, residue: (i, 0, 0)),
            scratch_shapes=[pltpu.VMEM((features, width), jnp.bfloat16)],
        ),
        out_shape=pltpu.HBM((peers, rows, width), jnp.bfloat16),
        compiler_params=pltpu.CompilerParams(vmem_limit_bytes=PROJECT_VMEM),
        cost_estimate=pl.CostEstimate(
            flops=2 * peers * rows * features * width,
            bytes_accessed=2 * (peers * rows * (features + width) + features * width),
            transcendentals=0,
        ),
        name="project_keys",
    )(residue, tokens, *held)


def moved(block, target):
    return lax.ppermute(block, Z, [(z, target(z) % PLANES) for z in range(PLANES)])


def shards(
    hidden_in, norm_gain, key_weight, fragment_index, outer_params, outer_moment, inner_params
):
    replicas = 4
    packed, scale = pack(hidden_in[0], norm_gain[None])
    packed, block = lax.optimization_barrier((packed, key_weight[0]))
    tokens = lax.all_to_all(packed, PLANE, 0, 0, tiled=True)
    own = lax.all_gather(block, "zh", axis=0, tiled=True)
    held = (
        own,
        moved(own, lambda z: z - 1),
        moved(own, lambda z: z + 1),
        moved(own, lambda z: z + 2 if z % 2 == 0 else z - 2),
    )
    _, fragment_index = lax.optimization_barrier((own, fragment_index))
    layer_idx = fragment_index[0]
    outer_layer = lax.dynamic_index_in_dim(outer_params, layer_idx, 0, keepdims=False)
    inner_layer = lax.dynamic_index_in_dim(inner_params[0], layer_idx, 0, keepdims=False)
    pseudo_grad = (outer_layer - inner_layer.astype(jnp.float32)).astype(jnp.bfloat16)
    residue = lax.axis_index("zl").astype(jnp.int32)[None]
    partial = project(residue, tokens, held)
    partial, layer_idx, pseudo_grad = lax.optimization_barrier((partial, layer_idx, pseudo_grad))
    partial = lax.all_to_all(partial, PLANE, 0, 0, tiled=True)
    outer_layer = lax.dynamic_index_in_dim(outer_params, layer_idx, 0, keepdims=False)
    moment_layer = lax.dynamic_index_in_dim(outer_moment, layer_idx, 0, keepdims=False)
    inner_layer = lax.dynamic_index_in_dim(inner_params[0], layer_idx, 0, keepdims=False)
    parts = [pseudo_grad.astype(jnp.float32)]
    for other in range(1, replicas):
        pairs = [(replica, replica ^ other) for replica in range(replicas)]
        parts.append(lax.ppermute(pseudo_grad, REP, pairs).astype(jnp.float32))
    summed = (parts[0] + parts[1]) + (parts[2] + parts[3])
    new_outer, new_moment = outer_update(summed / replicas, outer_layer, moment_layer)
    mixed_inner = (
        mix_keep * inner_layer.astype(jnp.float32) + (1.0 - mix_keep) * new_outer
    ).astype(jnp.bfloat16)
    keys = (jnp.sum(partial.astype(jnp.float32), axis=0) * scale).astype(jnp.bfloat16)
    return (keys[None], new_outer, new_moment, mixed_inner[None])


def solution(mesh):
    fine = Mesh(mesh.devices.reshape(2, 2, 4, 4, 2, 4), ("yl", "core", "zh", "zl", "yh", "x"))
    fsdp = ("zh", "zl", "yh", "x")
    placed = (
        P(REP, fsdp, None),
        P(),
        P(REP, fsdp, None),
        P(),
        P(None, fsdp, None),
        P(None, fsdp, None),
        P(REP, None, fsdp, None),
    )
    return jax.shard_map(
        shards,
        mesh=fine,
        in_specs=placed,
        out_specs=(
            P(REP, fsdp, None),
            P(fsdp, None),
            P(fsdp, None),
            P(REP, fsdp, None),
        ),
        check_vma=False,
    )
```

```python
import jax
import jax.numpy as jnp
from jax import lax
from jax.experimental import pallas as pl
from jax.experimental.pallas import tpu as pltpu
from jax.sharding import Mesh, PartitionSpec as P

momentum_coef = 0.9
outer_rate = 0.7
mix_keep = 0.5
epsilon = 1e-05

Z, PLANE, REP = ("zh", "zl"), ("yh", "x"), ("yl", "core")
PLANES, PEERS = 16, 8
ROWS, SOURCES = 96, 4
PACK_VMEM, PROJECT_VMEM = 60 * 1024 * 1024, 24 * 1024 * 1024


def outer_update(averaged, outer_layer, moment_layer):
    new_moment = momentum_coef * moment_layer + averaged
    new_outer = outer_layer - outer_rate * (averaged + momentum_coef * new_moment)
    return (new_outer, new_moment)


def pack_kernel(hidden_ref, gain_ref, packed_ref, scale_ref):
    hidden = hidden_ref[...].astype(jnp.float32)
    features = hidden.shape[1]
    mean_square = jnp.sum(hidden * hidden, axis=-1, keepdims=True) / features
    scale_ref[...] = lax.rsqrt(mean_square + epsilon)
    gained = hidden * gain_ref[...]
    low = lax.broadcasted_iota(jnp.int32, (hidden.shape[0], 128), 1) < 64
    for pair in range(PLANES // 2):
        for tile in range(PEERS // 2):
            start = pair * 1024 + tile * 128
            first = gained[:, start : start + 128]
            second = gained[:, start + 512 : start + 640]
            columns = slice(pair * 128, pair * 128 + 128)
            even = jnp.where(low, first, pltpu.roll(second, 64, 1))
            odd = jnp.where(low, pltpu.roll(first, 64, 1), second)
            packed_ref[2 * tile, :, columns] = even.astype(jnp.bfloat16)
            packed_ref[2 * tile + 1, :, columns] = odd.astype(jnp.bfloat16)


def pack(hidden, gain):
    tokens, features = hidden.shape
    return pl.pallas_call(
        pack_kernel,
        grid=(tokens // ROWS,),
        in_specs=[
            pl.BlockSpec((ROWS, features), lambda i: (i, 0)),
            pl.BlockSpec((1, features), lambda i: (0, 0)),
        ],
        out_specs=[
            pl.BlockSpec((PEERS, ROWS, features // PEERS), lambda i: (0, i, 0)),
            pl.BlockSpec((ROWS, 1), lambda i: (i, 0)),
        ],
        out_shape=[
            pltpu.HBM((PEERS, tokens, features // PEERS), jnp.bfloat16),
            jax.ShapeDtypeStruct((tokens, 1), jnp.float32),
        ],
        compiler_params=pltpu.CompilerParams(vmem_limit_bytes=PACK_VMEM),
        cost_estimate=pl.CostEstimate(
            flops=4 * tokens * features, bytes_accessed=4 * tokens * features, transcendentals=tokens
        ),
        name="pack_hidden",
    )(hidden, gain)


STEPS = 4
HELD = (0, 1, -1, 2)


def project_kernel(residue_ref, tokens_ref, *refs):
    held_refs, (out_ref, weight) = refs[: len(HELD)], refs[len(HELD) :]

    @pl.when(pl.program_id(0) == 0)
    def _():
        for held_ref, above in zip(held_refs, HELD, strict=True):
            residue = lax.rem(residue_ref[0] + above + STEPS, STEPS)
            for at in range(PLANES // STEPS):
                rows = pl.ds(pl.multiple_of((at * STEPS + residue) * 64, 64), 64)
                weight[rows, :] = held_ref[at * 64 : at * 64 + 64, :]

    tokens = tokens_ref[...].reshape(-1, tokens_ref.shape[-1])
    product = jnp.dot(tokens, weight[...], preferred_element_type=jnp.float32)
    out_ref[...] = product.astype(jnp.bfloat16).reshape(out_ref.shape)


def project(residue, tokens, held):
    peers, rows, features = tokens.shape
    width = held[0].shape[1]
    whole = [pl.BlockSpec(part.shape, lambda i, residue: (0, 0)) for part in held]
    return pl.pallas_call(
        project_kernel,
        grid_spec=pltpu.PrefetchScalarGridSpec(
            num_scalar_prefetch=1,
            grid=(peers // SOURCES,),
            in_specs=[pl.BlockSpec((SOURCES, rows, features), lambda i, residue: (i, 0, 0)), *whole],
            out_specs=pl.BlockSpec((SOURCES, rows, width), lambda i, residue: (i, 0, 0)),
            scratch_shapes=[pltpu.VMEM((features, width), jnp.bfloat16)],
        ),
        out_shape=pltpu.HBM((peers, rows, width), jnp.bfloat16),
        compiler_params=pltpu.CompilerParams(vmem_limit_bytes=PROJECT_VMEM),
        cost_estimate=pl.CostEstimate(
            flops=2 * peers * rows * features * width,
            bytes_accessed=2 * (peers * rows * (features + width) + features * width),
            transcendentals=0,
        ),
        name="project_keys",
    )(residue, tokens, *held)


def moved(block, target):
    return lax.ppermute(block, Z, [(z, target(z) % PLANES) for z in range(PLANES)])


def swapped(block, axis):
    return lax.ppermute(block, axis, [(0, 1), (1, 0)])


def shards(
    hidden_in, norm_gain, key_weight, fragment_index, outer_params, outer_moment, inner_params
):
    replicas = 4
    packed, scale = pack(hidden_in[0], norm_gain[None])
    packed, block = lax.optimization_barrier((packed, key_weight[0]))
    tokens = lax.all_to_all(packed, PLANE, 0, 0, tiled=True)
    own = lax.all_gather(block, "zh", axis=0, tiled=True)
    held = [
        own,
        moved(own, lambda z: z - 1),
        moved(own, lambda z: z + 1),
        moved(own, lambda z: z + 2 if z % 2 == 0 else z - 2),
    ]
    held[0], fragment_index = lax.optimization_barrier((own, fragment_index))
    layer_idx = fragment_index[0]
    outer_layer = lax.dynamic_index_in_dim(outer_params, layer_idx, 0, keepdims=False)
    inner_layer = lax.dynamic_index_in_dim(inner_params[0], layer_idx, 0, keepdims=False)
    pseudo_grad = (outer_layer - inner_layer.astype(jnp.float32)).astype(jnp.bfloat16)
    pair_sum = pseudo_grad.astype(jnp.float32) + swapped(pseudo_grad, "core").astype(jnp.float32)
    pair_sum = pair_sum.astype(jnp.bfloat16)
    other_sum = swapped(pair_sum, "yl")
    residue = lax.axis_index("zl").astype(jnp.int32)[None]
    partial = project(residue, tokens, held)
    partial, layer_idx, pair_sum, other_sum = lax.optimization_barrier(
        (partial, layer_idx, pair_sum, other_sum)
    )
    partial = lax.all_to_all(partial, PLANE, 0, 0, tiled=True)
    outer_layer = lax.dynamic_index_in_dim(outer_params, layer_idx, 0, keepdims=False)
    moment_layer = lax.dynamic_index_in_dim(outer_moment, layer_idx, 0, keepdims=False)
    inner_layer = lax.dynamic_index_in_dim(inner_params[0], layer_idx, 0, keepdims=False)
    summed = pair_sum.astype(jnp.float32) + other_sum.astype(jnp.float32)
    new_outer, new_moment = outer_update(summed / replicas, outer_layer, moment_layer)
    mixed_inner = (
        mix_keep * inner_layer.astype(jnp.float32) + (1.0 - mix_keep) * new_outer
    ).astype(jnp.bfloat16)
    keys = (jnp.sum(partial.astype(jnp.float32), axis=0) * scale).astype(jnp.bfloat16)
    return (keys[None], new_outer, new_moment, mixed_inner[None])


def solution(mesh):
    fine = Mesh(mesh.devices.reshape(2, 2, 4, 4, 2, 4), ("yl", "core", "zh", "zl", "yh", "x"))
    fsdp = ("zh", "zl", "yh", "x")
    placed = (
        P(REP, fsdp, None),
        P(),
        P(REP, fsdp, None),
        P(),
        P(None, fsdp, None),
        P(None, fsdp, None),
        P(REP, None, fsdp, None),
    )
    return jax.shard_map(
        shards,
        mesh=fine,
        in_specs=placed,
        out_specs=(
            P(REP, fsdp, None),
            P(fsdp, None),
            P(fsdp, None),
            P(REP, fsdp, None),
        ),
        check_vma=False,
    )
```

```python
import jax
import jax.numpy as jnp
from jax import lax
from jax.experimental import pallas as pl
from jax.experimental.pallas import tpu as pltpu
from jax.sharding import Mesh, PartitionSpec as P

momentum_coef = 0.9
outer_rate = 0.7
mix_keep = 0.5
epsilon = 1e-05

Z, PLANE, REP = ("zh", "zl"), ("yh", "x"), ("yl", "core")
PLANES, PEERS = 16, 8
ROWS, SOURCES = 96, 4
PACK_VMEM, PROJECT_VMEM = 60 * 1024 * 1024, 24 * 1024 * 1024


def outer_update(averaged, outer_layer, moment_layer):
    new_moment = momentum_coef * moment_layer + averaged
    new_outer = outer_layer - outer_rate * (averaged + momentum_coef * new_moment)
    return (new_outer, new_moment)


def pack_kernel(hidden_ref, gain_ref, packed_ref, scale_ref):
    hidden = hidden_ref[...].astype(jnp.float32)
    features = hidden.shape[1]
    mean_square = jnp.sum(hidden * hidden, axis=-1, keepdims=True) / features
    scale_ref[...] = lax.rsqrt(mean_square + epsilon)
    gained = hidden * gain_ref[...]
    low = lax.broadcasted_iota(jnp.int32, (hidden.shape[0], 128), 1) < 64
    for pair in range(PLANES // 2):
        for tile in range(PEERS // 2):
            start = pair * 1024 + tile * 128
            first = gained[:, start : start + 128]
            second = gained[:, start + 512 : start + 640]
            columns = slice(pair * 128, pair * 128 + 128)
            even = jnp.where(low, first, pltpu.roll(second, 64, 1))
            odd = jnp.where(low, pltpu.roll(first, 64, 1), second)
            packed_ref[2 * tile, :, columns] = even.astype(jnp.bfloat16)
            packed_ref[2 * tile + 1, :, columns] = odd.astype(jnp.bfloat16)


def pack(hidden, gain):
    tokens, features = hidden.shape
    return pl.pallas_call(
        pack_kernel,
        grid=(tokens // ROWS,),
        in_specs=[
            pl.BlockSpec((ROWS, features), lambda i: (i, 0)),
            pl.BlockSpec((1, features), lambda i: (0, 0)),
        ],
        out_specs=[
            pl.BlockSpec((PEERS, ROWS, features // PEERS), lambda i: (0, i, 0)),
            pl.BlockSpec((ROWS, 1), lambda i: (i, 0)),
        ],
        out_shape=[
            pltpu.HBM((PEERS, tokens, features // PEERS), jnp.bfloat16),
            jax.ShapeDtypeStruct((tokens, 1), jnp.float32),
        ],
        compiler_params=pltpu.CompilerParams(vmem_limit_bytes=PACK_VMEM),
        cost_estimate=pl.CostEstimate(
            flops=4 * tokens * features, bytes_accessed=4 * tokens * features, transcendentals=tokens
        ),
        name="pack_hidden",
    )(hidden, gain)


STEPS = 4
HELD = (0, 1, -1, 2)


def project_kernel(residue_ref, tokens_ref, *refs):
    held_refs, (out_ref, weight) = refs[: len(HELD)], refs[len(HELD) :]

    @pl.when(pl.program_id(0) == 0)
    def _():
        for held_ref, above in zip(held_refs, HELD, strict=True):
            residue = lax.rem(residue_ref[0] + above + STEPS, STEPS)
            for at in range(PLANES // STEPS):
                rows = pl.ds(pl.multiple_of((at * STEPS + residue) * 64, 64), 64)
                weight[rows, :] = held_ref[at * 64 : at * 64 + 64, :]

    tokens = tokens_ref[...].reshape(-1, tokens_ref.shape[-1])
    product = jnp.dot(tokens, weight[...], preferred_element_type=jnp.float32)
    out_ref[...] = product.astype(jnp.bfloat16).reshape(out_ref.shape)


def project(residue, tokens, held):
    peers, rows, features = tokens.shape
    width = held[0].shape[1]
    whole = [pl.BlockSpec(part.shape, lambda i, residue: (0, 0)) for part in held]
    return pl.pallas_call(
        project_kernel,
        grid_spec=pltpu.PrefetchScalarGridSpec(
            num_scalar_prefetch=1,
            grid=(peers // SOURCES,),
            in_specs=[pl.BlockSpec((SOURCES, rows, features), lambda i, residue: (i, 0, 0)), *whole],
            out_specs=pl.BlockSpec((SOURCES, rows, width), lambda i, residue: (i, 0, 0)),
            scratch_shapes=[pltpu.VMEM((features, width), jnp.bfloat16)],
        ),
        out_shape=pltpu.HBM((peers, rows, width), jnp.bfloat16),
        compiler_params=pltpu.CompilerParams(vmem_limit_bytes=PROJECT_VMEM),
        cost_estimate=pl.CostEstimate(
            flops=2 * peers * rows * features * width,
            bytes_accessed=2 * (peers * rows * (features + width) + features * width),
            transcendentals=0,
        ),
        name="project_keys",
    )(residue, tokens, *held)


def moved(block, target):
    return lax.ppermute(block, Z, [(z, target(z) % PLANES) for z in range(PLANES)])


def shards(
    hidden_in, norm_gain, key_weight, fragment_index, outer_params, outer_moment, inner_params
):
    replicas = 4
    packed, scale = pack(hidden_in[0], norm_gain[None])
    packed, block = lax.optimization_barrier((packed, key_weight[0]))
    tokens = lax.all_to_all(packed, PLANE, 0, 0, tiled=True)
    own = lax.all_gather(block, "zh", axis=0, tiled=True)
    held = (
        own,
        moved(own, lambda z: z - 1),
        moved(own, lambda z: z + 1),
        moved(own, lambda z: z + 2 if z % 2 == 0 else z - 2),
    )
    _, fragment_index = lax.optimization_barrier((own, fragment_index))
    layer_idx = fragment_index[0]
    outer_layer = lax.dynamic_index_in_dim(outer_params, layer_idx, 0, keepdims=False)
    inner_layer = lax.dynamic_index_in_dim(inner_params[0], layer_idx, 0, keepdims=False)
    pseudo_grad = (outer_layer - inner_layer.astype(jnp.float32)).astype(jnp.bfloat16)
    residue = lax.axis_index("zl").astype(jnp.int32)[None]
    partial = project(residue, tokens, held)
    partial, layer_idx, pseudo_grad = lax.optimization_barrier((partial, layer_idx, pseudo_grad))
    partial = lax.all_to_all(partial, PLANE, 0, 0, tiled=True)
    outer_layer = lax.dynamic_index_in_dim(outer_params, layer_idx, 0, keepdims=False)
    moment_layer = lax.dynamic_index_in_dim(outer_moment, layer_idx, 0, keepdims=False)
    inner_layer = lax.dynamic_index_in_dim(inner_params[0], layer_idx, 0, keepdims=False)
    every = lax.all_gather(pseudo_grad, REP, axis=0, tiled=False).astype(jnp.float32)
    summed = (every[0] + every[1]) + (every[2] + every[3])
    new_outer, new_moment = outer_update(summed / replicas, outer_layer, moment_layer)
    mixed_inner = (
        mix_keep * inner_layer.astype(jnp.float32) + (1.0 - mix_keep) * new_outer
    ).astype(jnp.bfloat16)
    keys = (jnp.sum(partial.astype(jnp.float32), axis=0) * scale).astype(jnp.bfloat16)
    return (keys[None], new_outer, new_moment, mixed_inner[None])


def solution(mesh):
    fine = Mesh(mesh.devices.reshape(2, 2, 4, 4, 2, 4), ("yl", "core", "zh", "zl", "yh", "x"))
    fsdp = ("zh", "zl", "yh", "x")
    placed = (
        P(REP, fsdp, None),
        P(),
        P(REP, fsdp, None),
        P(),
        P(None, fsdp, None),
        P(None, fsdp, None),
        P(REP, None, fsdp, None),
    )
    return jax.shard_map(
        shards,
        mesh=fine,
        in_specs=placed,
        out_specs=(
            P(REP, fsdp, None),
            P(fsdp, None),
            P(fsdp, None),
            P(REP, fsdp, None),
        ),
        check_vma=False,
    )
```
